128 devices in a mesh: ctx: 32 (over z, y, x_hi), fsdp: 4 (over x_lo, core).
Axes of the slice: x: 4 (x_hi: 2, x_lo: 2; x = x_hi * 2 + x_lo), y: 4, z: 4, core: 2. Of those that a mesh axis runs over, the one named last changes fastest.
Arguments:
- inputs: bfloat16 [4, 4096, 768], P('fsdp', 'ctx'), may hold values from -6 to 6
- qkv_weight: bfloat16 [1, 768, 2304], P(None, ('ctx', 'fsdp')), may hold values from -0.3125 to 0.3125
- qkv_bias: bfloat16 [1, 2304], P(None, ('ctx', 'fsdp')), may hold values from -3 to 3
- out_weight: bfloat16 [1, 768, 768], P(None, ('ctx', 'fsdp')), may hold values from -1.75 to 1.75
- out_bias: bfloat16 [1, 768], P(None, ('ctx', 'fsdp')), may hold values from -3 to 3
- up_weight: bfloat16 [1, 768, 3072], P(None, ('ctx', 'fsdp')), may hold values from -0.21875 to 0.21875
- up_bias: bfloat16 [1, 3072], P(None, ('ctx', 'fsdp')), may hold values from -3 to 3
- down_weight: bfloat16 [1, 3072, 768], P(None, ('ctx', 'fsdp')), may hold values from -0.109375 to 0.109375
- down_bias: bfloat16 [1, 768], P(None, ('ctx', 'fsdp')), may hold values from -3 to 3
- attn_gain: bfloat16 [1, 768], P(None, ('ctx', 'fsdp')), may hold values from 0.099609375 to 1.8984375
- attn_shift: bfloat16 [1, 768], P(None, ('ctx', 'fsdp')), may hold values from -2 to 2
- mlp_gain: bfloat16 [1, 768], P(None, ('ctx', 'fsdp')), may hold values from 0.099609375 to 1.8984375
- mlp_shift: bfloat16 [1, 768], P(None, ('ctx', 'fsdp')), may hold values from -2 to 2
- cotangent: bfloat16 [4, 4096, 768], P('fsdp', 'ctx'), may hold values from -6 to 6
Outputs:
- outputs: bfloat16 [4, 4096, 768], P('fsdp', 'ctx')
- input_grad: float32 [4, 4096, 768], P('fsdp', 'ctx')
- qkv_weight_grad: float32 [1, 768, 2304], P(None, ('ctx', 'fsdp'))
- qkv_bias_grad: float32 [1, 2304], P(None, ('ctx', 'fsdp'))
- out_weight_grad: float32 [1, 768, 768], P(None, ('ctx', 'fsdp'))
- out_bias_grad: float32 [1, 768], P(None, ('ctx', 'fsdp'))
- up_weight_grad: float32 [1, 768, 3072], P(None, ('ctx', 'fsdp'))
- up_bias_grad: float32 [1, 3072], P(None, ('ctx', 'fsdp'))
- down_weight_grad: float32 [1, 3072, 768], P(None, ('ctx', 'fsdp'))
- down_bias_grad: float32 [1, 768], P(None, ('ctx', 'fsdp'))
- attn_gain_grad: float32 [1, 768], P(None, ('ctx', 'fsdp'))
- attn_shift_grad: float32 [1, 768], P(None, ('ctx', 'fsdp'))
- mlp_gain_grad: float32 [1, 768], P(None, ('ctx', 'fsdp'))
- mlp_shift_grad: float32 [1, 768], P(None, ('ctx', 'fsdp'))
The draws below stay inside these ranges and needn't reach their ends.
All inputs are finite; a program needn't handle non-finite values.
Results may differ from the reference program's by a relative error of at most 0.01225.
The reference program's roundings to bfloat16 on the way count: a program that leaves them out, or rounds other values in their place, can miss the bound.
Values may be sent and summed in bfloat16 or wider, within the bound.
A program may use at most 192 MiB of HBM per device.

```python
import jax
import jax.numpy as jnp
from jax import lax

D = 768
H = 12
HD = 64
FF = 3072
ROT = 16
LAYERS = 1
LEN = 4096
SEQS = 4


def shard_levels(own_key, dims, pieces, low, top_value):
    gain = 1.0
    for position, parts in pieces:
        steps = jax.random.uniform(jax.random.fold_in(jax.random.fold_in(own_key, 6), position), (parts,), jnp.float32, low / len(pieces), top_value / len(pieces))
        gain = gain * jnp.repeat(jnp.exp(steps), dims[position] // parts).reshape((-1,) + (1,) * (len(dims) - 1 - position))
    return gain


def noise(key, shape, scale, limit, pieces=(), held_as=jnp.bfloat16):
    gain = shard_levels(key, shape, pieces, -0.22, 0.18) if pieces else 1.0
    drawn = jax.random.normal(key, shape, jnp.float32) * scale * gain
    return jnp.minimum(jnp.maximum(drawn, -limit), limit).astype(held_as)


def setup_inputs(seed: int = 0) -> dict:
    key_of = jax.random.split(jax.random.key(seed), 15)
    return {
        "inputs": noise(key_of[0], (SEQS, LEN, D), 1.0, 6.0, ((0, 4), (1, 32))),
        "qkv_weight": noise(key_of[1], (LAYERS, D, 3 * D), (D // 2) ** -0.5, 0.3125, ((1, 128),)),
        "qkv_bias": noise(key_of[2], (LAYERS, 3 * D), 0.5, 3.0, ((1, 128),)),
        "out_weight": noise(key_of[3], (LAYERS, D, D), (max(1, D // 64)) ** -0.5, 1.75, ((1, 128),)),
        "out_bias": noise(key_of[4], (LAYERS, D), 0.5, 3.0, ((1, 128),)),
        "up_weight": noise(key_of[5], (LAYERS, D, FF), D ** -0.5, 0.21875, ((1, 128),)),
        "up_bias": noise(key_of[6], (LAYERS, FF), 0.5, 3.0, ((1, 128),)),
        "down_weight": noise(key_of[7], (LAYERS, FF, D), FF ** -0.5, 0.109375, ((1, 128),)),
        "down_bias": noise(key_of[8], (LAYERS, D), 0.5, 3.0, ((1, 128),)),
        "attn_gain": jnp.clip(1.0 + 0.18 * jax.random.normal(key_of[9], (LAYERS, D), jnp.float32), 0.099609375, 1.8984375).astype(jnp.bfloat16),
        "attn_shift": noise(key_of[10], (LAYERS, D), 0.3, 2.0, ((1, 128),)),
        "mlp_gain": jnp.clip(1.0 + 0.18 * jax.random.normal(key_of[11], (LAYERS, D), jnp.float32), 0.099609375, 1.8984375).astype(jnp.bfloat16),
        "mlp_shift": noise(key_of[12], (LAYERS, D), 0.3, 2.0, ((1, 128),)),
        "cotangent": noise(key_of[13], (SEQS, LEN, D), 1.0, 6.0, ((0, 4), (1, 32))),
    }


@jax.custom_vjp
def low(v):
    return lax.optimization_barrier(v.astype(jnp.bfloat16)).astype(jnp.float32)

@jax.custom_vjp
def low_back(v):
    return v

def low_keep(v):
    return (low(v), None)

def low_pass(kept, grad):
    return (grad,)

def back_keep(v):
    return (v, None)

def back_low(kept, grad):
    return (low(grad),)
low.defvjp(low_keep, low_pass)
low_back.defvjp(back_keep, back_low)
score_scale = 0.125
far_below = -1e+30

def matmul_high(left, right):
    return jnp.dot(left, right, precision=lax.Precision.HIGHEST, preferred_element_type=jnp.float32)

def norm_rows(values, gain_row, shift_row):
    center = values - lax.optimization_barrier(jnp.mean(values, axis=-1, keepdims=True))
    spread = lax.optimization_barrier(jnp.mean(center * center, axis=-1, keepdims=True))
    return center * lax.rsqrt(spread + 1e-05) * gain_row + shift_row

def rotary_tables(positions):
    halves = ROT // 2
    frequency = 10000.0 ** (-2.0 * jnp.arange(halves, dtype=jnp.float32) / ROT)
    angle_table = positions[:, None] * frequency[None, :]
    return (jnp.cos(angle_table), jnp.sin(angle_table))

def rotate(heads_in, cosine_table, sinus_table):
    halves = ROT // 2
    front = heads_in[..., :halves]
    behind = heads_in[..., halves:ROT]
    cos_b = cosine_table[:, None, :]
    sin_b = sinus_table[:, None, :]
    return jnp.concatenate([front * cos_b - behind * sin_b, behind * cos_b + front * sin_b, heads_in[..., ROT:]], axis=-1)

def attend(queries, keys_all, values_all):
    block_rows = min(512, LEN)
    key_place = jnp.arange(LEN, dtype=jnp.int32)

    def one_block(block_index):
        query_part = lax.dynamic_slice_in_dim(queries, block_index * block_rows, block_rows, 0)
        scores = low_back(jnp.einsum('qhd,khd->hqk', query_part, keys_all, precision=lax.Precision.HIGHEST) * score_scale)
        query_place = block_index * block_rows + jnp.arange(block_rows, dtype=jnp.int32)
        allowed = key_place[None, :] <= query_place[:, None]
        scores = jnp.where(allowed[None], scores, far_below)
        weights = jnp.exp(scores - jax.nn.logsumexp(scores, axis=-1, keepdims=True))
        return jnp.einsum('hqk,khd->qhd', weights, values_all, precision=lax.Precision.HIGHEST)
    blocks_out = lax.map(jax.checkpoint(one_block), jnp.arange(LEN // block_rows, dtype=jnp.int32))
    return blocks_out.reshape(LEN, H * HD)

def layer(residual, params, cosine_table, sinus_table):
    w_qkv, b_qkv, w_out, b_out, w_up, b_up, w_down, b_down, gain_attn, shift_attn, gain_mlp, shift_mlp = params
    normed_attn = low(norm_rows(residual, gain_attn, shift_attn))
    normed_mlp = low(norm_rows(residual, gain_mlp, shift_mlp))
    qkv_rows = low_back(matmul_high(normed_attn, w_qkv) + b_qkv).reshape(LEN, 3, H, HD)
    queries = low(rotate(qkv_rows[:, 0], cosine_table, sinus_table))
    keys_all = low(rotate(qkv_rows[:, 1], cosine_table, sinus_table))
    values_all = low(qkv_rows[:, 2])
    attended = low(low_back(attend(queries, keys_all, values_all)))
    branch_attn = low_back(matmul_high(attended, w_out) + b_out)
    upper = low_back(matmul_high(normed_mlp, w_up) + b_up)
    gelu_low = low(jax.nn.gelu(upper, approximate=False))
    branch_mlp = low_back(matmul_high(gelu_low, w_down) + b_down)
    return residual + branch_attn + branch_mlp

def forward(sequences, params):
    cosine_table, sinus_table = rotary_tables(jnp.arange(LEN, dtype=jnp.float32))

    def per_sequence(residual):
        for layer_index in range(LAYERS):
            residual = layer(residual, tuple((member[layer_index] for member in params)), cosine_table, sinus_table)
        return residual
    return lax.map(per_sequence, sequences)

def reference(inputs, qkv_weight, qkv_bias, out_weight, out_bias, up_weight, up_bias, down_weight, down_bias, attn_gain, attn_shift, mlp_gain, mlp_shift, cotangent):
    params = tuple((member.astype(jnp.float32) for member in (qkv_weight, qkv_bias, out_weight, out_bias, up_weight, up_bias, down_weight, down_bias, attn_gain, attn_shift, mlp_gain, mlp_shift)))
    outputs, pullback = jax.vjp(forward, inputs.astype(jnp.float32), params)
    input_grad, weight_grads = pullback(cotangent.astype(jnp.float32))
    return (outputs.astype(jnp.bfloat16), input_grad, weight_grads[0], weight_grads[1], weight_grads[2], weight_grads[3], weight_grads[4], weight_grads[5], weight_grads[6], weight_grads[7], weight_grads[8], weight_grads[9], weight_grads[10], weight_grads[11])
```

```python
import functools

import jax
import jax.numpy as jnp
import numpy as np
from jax import lax
from jax.experimental import pallas as pl
from jax.experimental.pallas import tpu as pltpu
from jax.sharding import PartitionSpec as P

F32 = jnp.float32
BF16 = jnp.bfloat16
MESH = pl.DeviceIdType.MESH
VMEM = pl.BlockSpec(memory_space=pltpu.VMEM)
HBM = pl.BlockSpec(memory_space=pl.ANY)
MIB = 1024 * 1024

UP, KV, Q, A = 768, 384, 256, 1408
B = 768
W = A + B


def place():
    ctx, fs = lax.axis_index("ctx"), lax.axis_index("fsdp")
    z, y, xh = ctx // 8, (ctx // 2) % 4, ctx % 2
    xl, c = fs // 2, fs % 2
    return z, y, xh, xl, c


def dev(z, y, x, c):
    return (z * 8 + y * 2 + x // 2, (x % 2) * 2 + c)


def rcopy(src, dst, ss, rs, to):
    return pltpu.make_async_remote_copy(
        src_ref=src, dst_ref=dst, send_sem=ss, recv_sem=rs, device_id=to, device_id_type=MESH
    )


def mm(a, b):
    return jnp.dot(a, b, preferred_element_type=F32)


def mm_nt(a, b):
    return lax.dot_general(a, b, (((1,), (1,)), ((), ())), preferred_element_type=F32)


def mm_tn(a, b):
    return lax.dot_general(a, b, (((0,), (0,)), ((), ())), preferred_element_type=F32)


def params(**kw):
    return pltpu.CompilerParams(vmem_limit_bytes=60 * MIB, **kw)


def gather_kernel(
    x_ref, g_ref, wz_ref, wb_ref, xa, ga, wa, zbuf, chunk,
    sw_s, sw_r, loc, tz_s, tz_r, wz_s, wz_r, s1_s, s2_s, s3_s, ring_r, part_r,
):
    z, y, xh, xl, c = place()
    x = xh * 2 + xl
    swap_to = dev(z, y, c * 2 + xl, xh)
    zpeer = [dev((z + k) % 4, y, x, c) for k in range(4)]
    first = [dev(z, (y + k * c) % 4, (x + k * (1 - c)) % 4, c) for k in range(4)]
    second = [dev(z, (y + k * (1 - c)) % 4, (x + k * c) % 4, c) for k in range(4)]
    partner = dev(z, y, x, 1 - c)

    def slot(k1, k2):
        yy = (y + k1 * c + k2 * (1 - c)) % 4
        xx = (x + k1 * (1 - c) + k2 * c) % 4
        return yy * 8 + xx * 2 + c

    bar = pltpu.get_barrier_semaphore()
    for to in zpeer[1:] + first[1:] + second[1:] + [partner]:
        pl.semaphore_signal(bar, inc=1, device_id=to, device_id_type=MESH)

    @pl.when(xh != c)
    def _():
        pl.semaphore_signal(bar, inc=1, device_id=swap_to, device_id_type=MESH)

    pl.semaphore_wait(bar, 10 + (xh + c) % 2)

    zs = [rcopy(wz_ref.at[(z + k) % 4], zbuf.at[z], wz_s.at[k], wz_r.at[(4 - k) % 4], zpeer[k]) for k in range(1, 4)]
    for d in zs:
        d.start()
    swaps = [rcopy(x_ref, xa.at[z], sw_s.at[0], sw_r.at[0], swap_to),
             rcopy(g_ref, ga.at[z], sw_s.at[1], sw_r.at[1], swap_to)]
    stays = [pltpu.make_async_copy(x_ref, xa.at[z], loc.at[0]), pltpu.make_async_copy(g_ref, ga.at[z], loc.at[1])]

    @pl.when(xh != c)
    def _():
        swaps[0].start()
        swaps[1].start()

    @pl.when(xh == c)
    def _():
        stays[0].start()
        stays[1].start()

    zbuf[z] = wz_ref[z]
    chunk[:, A:] = wb_ref[...]
    for d in zs:
        d.wait()
    chunk[:, :A] = zbuf[...].reshape(32, A).astype(BF16)

    me = slot(0, 0)
    own = pltpu.make_async_copy(chunk, wa.at[me], loc.at[2])
    own.start()
    sends = []

    def send(src, where, ss, rs, to):
        d = rcopy(src, wa.at[where], ss, rs, to)
        d.start()
        sends.append(d)

    for k in range(1, 4):
        send(chunk, me, s1_s.at[k], ring_r.at[4 - k, 0], first[k])
    for k in range(1, 4):
        send(chunk, me, s2_s.at[0, k], ring_r.at[0, 4 - k], second[k])
    send(chunk, me, s3_s.at[0, 0], part_r.at[0, 0], partner)

    toks = []
    for t, arr in enumerate((xa, ga)):

        @pl.when(xh != c)
        def _():
            swaps[t].wait()

        @pl.when(xh == c)
        def _():
            stays[t].wait()

        for k in range(1, 4):
            d = rcopy(arr.at[z], arr.at[z], tz_s.at[t, k], tz_r.at[t, 4 - k], zpeer[k])
            d.start()
            toks.append(d)

    def arrived(k1, k2, rs):
        p = slot(k1, k2)
        rcopy(wa.at[p], wa.at[p], s3_s.at[k1, k2], rs, partner).wait_recv()
        return p

    for k1 in range(1, 4):
        p = arrived(k1, 0, ring_r.at[k1, 0])
        for k in range(1, 4):
            send(wa.at[p], p, s2_s.at[k1, k], ring_r.at[k1, 4 - k], second[k])
        send(wa.at[p], p, s3_s.at[k1, 0], part_r.at[k1, 0], partner)
    for k2 in range(1, 4):
        for k1 in range(4):
            p = arrived(k1, k2, ring_r.at[k1, k2])
            send(wa.at[p], p, s3_s.at[k1, k2], part_r.at[k1, k2], partner)
    for k1 in range(4):
        for k2 in range(4):
            arrived(k1, k2, part_r.at[k1, k2])
    for d in toks:
        d.wait()
    for d in sends:
        d.wait_send()
    own.wait()


def gather_all(x, g, wz, wb):
    dma = pltpu.SemaphoreType.DMA
    tok = jax.ShapeDtypeStruct((4, 128, 768), BF16)
    return pl.pallas_call(
        gather_kernel,
        out_shape=(tok, tok, jax.ShapeDtypeStruct((32, 32, W), BF16)),
        in_specs=[HBM, HBM, VMEM, VMEM],
        out_specs=(HBM, HBM, HBM),
        scratch_shapes=[
            pltpu.VMEM((4, 8, A), F32), pltpu.VMEM((32, W), BF16),
            dma((2,)), dma((2,)), dma((3,)), dma((2, 4)), dma((2, 4)), dma((4,)), dma((4,)),
            dma((4,)), dma((4, 4)), dma((4, 4)), dma((4, 4)), dma((4, 4)),
        ],
        compiler_params=params(collective_id=0, has_side_effects=True),
        name="gather_tokens_weights",
    )(x, g, wz, wb)


def turn(tile, cos, plus, minus):
    return tile * cos + pltpu.roll(tile, 8, 1) * plus + pltpu.roll(tile, 120, 1) * minus


def lanes_below(n):
    return lax.broadcasted_iota(jnp.int32, (128, 128), 1) < n


def front_kernel(
    x_ref, g_ref, w_ref, s_ref, s3_ref, vec_ref, qb_ref, cos_ref, sp_ref, sm_ref,
    kv_ref, qd_ref, na_ref, nm_ref, xh_ref, ow_ref, dw_ref, xp, qkv, dof, owf, dwf,
):
    xp[...] = mm(x_ref[...], s_ref[...])
    lane = lax.broadcasted_iota(jnp.int32, (1, 1024), 1)
    real = jnp.where(lane % 8 < 6, 1.0, 0.0).astype(F32)

    @pl.loop(0, 8)
    def _(i):
        r = pl.ds(pl.multiple_of(i * 64, 64), 64)
        v = xp[r, :]
        mean = jnp.sum(v, axis=1, keepdims=True) * (1.0 / 768.0)
        cen = (v - mean) * real
        var = jnp.sum(cen * cen, axis=1, keepdims=True) * (1.0 / 768.0)
        xh = cen * lax.rsqrt(var + 1e-5)
        xh_ref[r, :] = xh
        na_ref[r, :] = (xh * vec_ref[0:1, :] + vec_ref[1:2, :]).astype(BF16)
        nm_ref[r, :] = (xh * vec_ref[2:3, :] + vec_ref[3:4, :]).astype(BF16)

    qkv[...] = mm(na_ref[...], w_ref[:, :, UP:A].reshape(1024, A - UP)) + qb_ref[0:1, :]

    @pl.loop(0, 32)
    def _(p):
        rows = w_ref[p, :, A:].astype(F32)
        dwf[pl.ds(pl.multiple_of(p * 24, 8), 24), :] = rows[:24]
        owf[pl.ds(pl.multiple_of(p * 8, 8), 8), :] = rows[24:]

    ow_ref[...] = owf[...].astype(BF16)
    dw_ref[...] = dwf[...].astype(BF16)
    dof[...] = mm_nt(g_ref[...], ow_ref[...]).astype(BF16)
    for h in range(3):
        qd_ref[h, 512:, :] = mm_nt(dof[...], s3_ref[h]).astype(BF16)

    @pl.loop(0, 4)
    def _(i):
        r = pl.ds(pl.multiple_of(i * 128, 128), 128)
        cos, plus, minus = cos_ref[r, :], sp_ref[r, :], sm_ref[r, :]
        low = lanes_below(64)
        kc, kp, km = jnp.where(low, cos, 1.0), jnp.where(low, plus, 0.0), jnp.where(low, minus, 0.0)
        for h in range(3):
            kv_ref[h, r, :] = turn(qkv[r, 128 * h : 128 * h + 128], kc, kp, km).astype(BF16)
        q01 = turn(qkv[r, 384:512], cos, plus, minus).astype(BF16).astype(F32) * 0.125
        q2 = turn(qkv[r, 512:640], cos, plus, minus).astype(BF16).astype(F32) * 0.125
        qd_ref[0, r, :] = jnp.where(low, q01, 0.0).astype(BF16)
        qd_ref[1, r, :] = jnp.where(low, pltpu.roll(q01, 64, 1), 0.0).astype(BF16)
        qd_ref[2, r, :] = jnp.where(low, q2, 0.0).astype(BF16)


def front(x, g, w, s, s3, vec, qb, cos, plus, minus):
    sh = jax.ShapeDtypeStruct
    return pl.pallas_call(
        front_kernel,
        out_shape=(
            sh((3, 512, 128), BF16), sh((3, 1024, 128), BF16), sh((512, 1024), BF16), sh((512, 1024), BF16),
            sh((512, 1024), F32), sh((256, 768), BF16), sh((768, 768), BF16),
        ),
        in_specs=[VMEM] * 10,
        out_specs=(VMEM,) * 7,
        scratch_shapes=[
            pltpu.VMEM((512, 1024), F32), pltpu.VMEM((512, 640), F32), pltpu.VMEM((512, 256), BF16),
            pltpu.VMEM((256, 768), F32), pltpu.VMEM((768, 768), F32),
        ],
        compiler_params=params(),
        name="norms_qkv",
    )(x, g, w, s, s3, vec, qb, cos, plus, minus)


def mlp_kernel(
    nm_ref, g_ref, w_ref, dw_ref, xh_ref, vec_ref, ub_ref,
    part_ref, dxh_ref, gs_ref, dub_ref, dwup_ref, dwd_ref, up, hid, du,
):
    wup = w_ref[:, :, :UP].reshape(1024, UP)
    up[...] = mm(nm_ref[...], wup) + ub_ref[0:1, :]
    gs_ref[...] = jnp.zeros((8, 1024), F32)
    dub_ref[...] = jnp.zeros((8, UP), F32)

    @pl.loop(0, 8)
    def _(i):
        r = pl.ds(pl.multiple_of(i * 64, 64), 64)
        u = up[r, :]
        cdf = 0.5 * (1.0 + lax.erf(u * np.float32(np.sqrt(0.5))))
        pdf = jnp.exp(-0.5 * u * u) * np.float32(1.0 / np.sqrt(2.0 * np.pi))
        hid[r, :] = (u * cdf).astype(BF16)
        up[r, :] = cdf + u * pdf

    part_ref[...] = mm(hid[...], dw_ref[...])

    @pl.loop(0, 4)
    def _(i):
        r = pl.ds(pl.multiple_of(i * 128, 128), 128)
        d = (mm_nt(g_ref[r, :], dw_ref[...]) * up[r, :]).astype(BF16)
        du[r, :] = d
        dub_ref[0:1, :] += jnp.sum(d.astype(F32), axis=0, keepdims=True)

    @pl.loop(0, 4)
    def _(i):
        r = pl.ds(pl.multiple_of(i * 128, 128), 128)
        dn = mm_nt(du[r, :], wup)
        gs_ref[0:1, :] += jnp.sum(dn * xh_ref[r, :], axis=0, keepdims=True)
        gs_ref[1:2, :] += jnp.sum(dn, axis=0, keepdims=True)
        dxh_ref[r, :] = dn * vec_ref[2:3, :]

    dwup_ref[...] = mm_tn(nm_ref[...], du[...]).astype(BF16)
    dwd_ref[...] = mm_tn(hid[...], g_ref[...])


def mlp(nm, g, w, dw, xh, vec, ub):
    sh = jax.ShapeDtypeStruct
    return pl.pallas_call(
        mlp_kernel,
        out_shape=(
            sh((512, 768), F32), sh((512, 1024), F32), sh((8, 1024), F32), sh((8, UP), F32),
            sh((1024, UP), BF16), sh((768, 768), F32),
        ),
        in_specs=[VMEM] * 7,
        out_specs=(VMEM,) * 6,
        scratch_shapes=[pltpu.VMEM((512, UP), F32), pltpu.VMEM((512, UP), BF16), pltpu.VMEM((512, UP), BF16)],
        compiler_params=params(),
        name="feed_forward",
    )(nm, g, w, dw, xh, vec, ub)


def kv_kernel(kv_ref, out, loc, y_s, y_r, p_s, p_r):
    z, y, xh, xl, c = place()
    x = xh * 2 + xl
    peer = [dev(z, (y + k) % 4, x, c) for k in range(4)]
    partner = dev(z, y, x, 1 - c)
    bar = pltpu.get_barrier_semaphore()
    for to in peer[1:] + [partner]:
        pl.semaphore_signal(bar, inc=1, device_id=to, device_id_type=MESH)
    pl.semaphore_wait(bar, 4)
    me = out.at[:, :, 2 * y + c]
    sends = [rcopy(kv_ref, me, y_s.at[k], y_r.at[4 - k], peer[k]) for k in range(1, 4)]
    sends.append(rcopy(kv_ref, me, p_s.at[0], p_r.at[0], partner))
    for d in sends:
        d.start()
    own = pltpu.make_async_copy(kv_ref, me, loc.at[0])
    own.start()
    for k in (1, 3, 2):
        there = out.at[:, :, 2 * ((y + k) % 4) + c]
        rcopy(there, there, y_s.at[k], y_r.at[k], peer[k]).wait_recv()
        d = rcopy(there, there, p_s.at[k], p_r.at[k], partner)
        d.start()
        sends.append(d)
    for k in range(4):
        there = out.at[:, :, 2 * ((y + k) % 4) + 1 - c]
        rcopy(there, there, p_s.at[k], p_r.at[k], partner).wait_recv()
    for d in sends:
        d.wait_send()
    own.wait()


def gather_kv(kv):
    dma = pltpu.SemaphoreType.DMA
    return pl.pallas_call(
        kv_kernel,
        out_shape=jax.ShapeDtypeStruct((3, 4, 8, 128, 128), BF16),
        in_specs=[HBM],
        out_specs=HBM,
        scratch_shapes=[dma((1,)), dma((4,)), dma((4,)), dma((4,)), dma((4,))],
        compiler_params=params(collective_id=1, has_side_effects=True),
        name="gather_keys_values",
    )(kv)


def attention_kernel(qd_ref, kv_ref, o_ref, dq_ref, dkv_ref, s_scr, top, tot, acc, delta):
    z, y, xh, xl, c = place()
    start = (2 * y + c) * 128
    row = start + lax.broadcasted_iota(jnp.int32, (128, 256), 0)
    key = lax.broadcasted_iota(jnp.int32, (128, 256), 1)

    def chunks(body):
        for j in range(4):

            @pl.loop(0, 4)
            def _(t):
                body(j, 128 * j, t, pl.ds(pl.multiple_of(1024 * j + t * 256, 256), 256))

    def twice(a):
        return jnp.concatenate([a, a], axis=1)

    @pl.loop(0, 3)
    def _(h):
        top[...] = jnp.full((512, 128), -1e30, F32)
        tot[...] = jnp.zeros((512, 128), F32)
        acc[...] = jnp.zeros((512, 128), F32)

        def scores(j, r0, t, keys):
            s = mm_nt(qd_ref[h, r0:512, :], kv_ref[h, keys, :])
            head = jnp.where(key + t * 256 <= row, s[:128], -1e30)
            s_scr[r0 : r0 + 128, keys] = head
            top[r0 : r0 + 128, :] = jnp.maximum(top[r0 : r0 + 128, :], jnp.maximum(head[:, :128], head[:, 128:]))
            if j < 3:
                rest = s[128:]
                s_scr[r0 + 128 :, keys] = rest
                top[r0 + 128 :, :] = jnp.maximum(top[r0 + 128 :, :], jnp.maximum(rest[:, :128], rest[:, 128:]))

        chunks(scores)
        top[...] = jnp.broadcast_to(jnp.max(top[...], axis=1, keepdims=True), (512, 128))

        def weigh(j, r0, t, keys):
            p = jnp.exp(s_scr[r0:, keys] - twice(top[r0:, :]))
            s_scr[r0:, keys] = p
            tot[r0:, :] += p[:, :128] + p[:, 128:]
            acc[r0:, :] += mm(p.astype(BF16), kv_ref[h, keys, :])

        chunks(weigh)
        inv = 1.0 / jnp.broadcast_to(jnp.sum(tot[...], axis=1, keepdims=True), (512, 128))
        tot[...] = inv
        att = acc[...] * inv
        o_ref[h] = att.astype(BF16)
        delta[...] = jnp.broadcast_to(
            jnp.sum(att * qd_ref[h, 512:, :].astype(F32), axis=1, keepdims=True), (512, 128)
        )
        acc[...] = jnp.zeros((512, 128), F32)

        def back(j, r0, t, keys):
            kv = kv_ref[h, keys, :]
            p = s_scr[r0:, keys] * twice(tot[r0:, :])
            dp = mm_nt(qd_ref[h, 512 + r0 :, :], kv)
            ds = (p * (dp - twice(delta[r0:, :]))).astype(BF16)
            acc[r0:, :] += mm(ds, kv)
            d = mm_tn(qd_ref[h, r0:512, :], ds) + mm_tn(qd_ref[h, 512 + r0 :, :], p.astype(BF16))
            dkv_ref[8 * j + 2 * t, h] = d[:, :128].astype(BF16)
            dkv_ref[8 * j + 2 * t + 1, h] = d[:, 128:].astype(BF16)

        chunks(back)
        dq_ref[h] = acc[...]


def attention(qd, kv):
    sh = jax.ShapeDtypeStruct
    return pl.pallas_call(
        attention_kernel,
        out_shape=(sh((3, 512, 128), BF16), sh((3, 512, 128), F32), sh((32, 3, 128, 128), BF16)),
        in_specs=[VMEM] * 2,
        out_specs=(VMEM,) * 3,
        scratch_shapes=[pltpu.VMEM((512, 4096), F32)] + [pltpu.VMEM((512, 128), F32)] * 4,
        compiler_params=params(),
        name="attention",
    )(qd, kv)


def dkv_kernel(dkv, out, buf1, buf2, pair, p_s, p_r, y_s, y_r):
    z, y, xh, xl, c = place()
    x = xh * 2 + xl
    peer = [dev(z, (y + k) % 4, x, c) for k in range(4)]
    partner = dev(z, y, x, 1 - c)
    bar = pltpu.get_barrier_semaphore()
    for to in peer[1:] + [partner]:
        pl.semaphore_signal(bar, inc=1, device_id=to, device_id_type=MESH)
    pl.semaphore_wait(bar, 4)
    order = (2, 1, 3, 0)
    halves = [rcopy(dkv.at[:, (y + k) % 4, 1 - c], buf1.at[k], p_s.at[k], p_r.at[k], partner) for k in range(4)]
    for k in order:
        halves[k].start()
    sends = []
    for k in order:
        halves[k].wait_recv()
        yy = (y + k) % 4

        @pl.loop(0, 4)
        def _(i):
            pair[k, i] = (dkv[i, yy, c].astype(F32) + buf1[k, i].astype(F32)).astype(BF16)

        if k:
            d = rcopy(pair.at[k], buf2.at[4 - k], y_s.at[k], y_r.at[4 - k], peer[k])
            d.start()
            sends.append(d)
    for k in range(1, 4):
        rcopy(pair.at[k], buf2.at[k], y_s.at[k], y_r.at[k], peer[k]).wait_recv()

    @pl.loop(0, 4)
    def _(i):
        out[i] = pair[0, i].astype(F32) + buf2[1, i].astype(F32) + buf2[2, i].astype(F32) + buf2[3, i].astype(F32)

    for d in halves + sends:
        d.wait_send()


def sum_dkv(dkv):
    dma = pltpu.SemaphoreType.DMA
    buf = pltpu.VMEM((4, 4, 3, 128, 128), BF16)
    return pl.pallas_call(
        dkv_kernel,
        out_shape=jax.ShapeDtypeStruct((4, 3, 128, 128), F32),
        in_specs=[VMEM],
        out_specs=VMEM,
        scratch_shapes=[buf, buf, buf, dma((4,)), dma((4,)), dma((4,)), dma((4,))],
        compiler_params=params(collective_id=2, has_side_effects=True),
        name="sum_key_value_grads",
    )(dkv)


def back_kernel(
    o_ref, dq_ref, dkv_ref, na_ref, xh_ref, g_ref, w_ref, ow_ref, part_ref, dxm_ref, dwd_ref, s_ref, s3_ref,
    vec_ref, ob_ref, cos_ref, sp_ref, sm_ref,
    outp_ref, dxp_ref, dwq_ref, dwb_ref, gs_ref, dqb_ref, dqkv, dxh, att, dwo,
):
    dqb_ref[...] = jnp.zeros((8, 640), F32)
    gs_ref[...] = jnp.zeros((8, 1024), F32)

    @pl.loop(0, 4)
    def _(i):
        r = pl.ds(pl.multiple_of(i * 128, 128), 128)
        cos, plus, minus = cos_ref[r, :], -sp_ref[r, :], -sm_ref[r, :]
        low = lanes_below(64)
        kc, kp, km = jnp.where(low, cos, 1.0), jnp.where(low, plus, 0.0), jnp.where(low, minus, 0.0)
        for h in range(3):
            dqkv[r, 128 * h : 128 * h + 128] = turn(dkv_ref[i, h].T, kc, kp, km).astype(BF16)
        d0, d1, d2 = dq_ref[0, r, :] * 0.125, dq_ref[1, r, :] * 0.125, dq_ref[2, r, :] * 0.125
        d01 = jnp.where(low, d0, pltpu.roll(d1, 64, 1))
        dqkv[r, 384:512] = turn(d01, cos, plus, minus).astype(BF16)
        dqkv[r, 512:640] = turn(jnp.where(low, d2, 0.0), cos, plus, minus).astype(BF16)
        dqb_ref[0:1, :] += jnp.sum(dqkv[r, :].astype(F32), axis=0, keepdims=True)

    wq = w_ref[:, :, UP:A].reshape(1024, A - UP)

    @pl.loop(0, 4)
    def _(i):
        r = pl.ds(pl.multiple_of(i * 128, 128), 128)
        dn = mm_nt(dqkv[r, :], wq)
        gs_ref[0:1, :] += jnp.sum(dn * xh_ref[r, :], axis=0, keepdims=True)
        gs_ref[1:2, :] += jnp.sum(dn, axis=0, keepdims=True)
        dxh[r, :] = (dxm_ref[r, :] + dn * vec_ref[0:1, :]).astype(BF16)

    dxp_ref[...] = mm_nt(dxh[...], s_ref[...]).astype(BF16)
    dwq_ref[...] = mm_tn(na_ref[...], dqkv[...]).astype(BF16)
    att[...] = (mm(o_ref[0], s3_ref[0]) + mm(o_ref[1], s3_ref[1]) + mm(o_ref[2], s3_ref[2])).astype(BF16)
    outp_ref[...] = (part_ref[...] + mm(att[...], ow_ref[...]) + ob_ref[0:1, :]).astype(BF16)
    dwo[...] = mm_tn(att[...], g_ref[...])

    @pl.loop(0, 32)
    def _(p):
        rows = jnp.concatenate(
            [dwd_ref[pl.ds(pl.multiple_of(p * 24, 8), 24), :], dwo[pl.ds(pl.multiple_of(p * 8, 8), 8), :]], axis=0
        )
        dwb_ref[p] = rows.astype(BF16)


def back(*args):
    sh = jax.ShapeDtypeStruct
    return pl.pallas_call(
        back_kernel,
        out_shape=(
            sh((512, 768), BF16), sh((512, 768), BF16), sh((1024, 640), BF16), sh((32, 32, 768), BF16),
            sh((8, 1024), F32), sh((8, 640), F32),
        ),
        in_specs=[VMEM] * 18,
        out_specs=(VMEM,) * 6,
        scratch_shapes=[
            pltpu.VMEM((512, 640), BF16), pltpu.VMEM((512, 1024), BF16), pltpu.VMEM((512, 256), BF16),
            pltpu.VMEM((256, 768), F32),
        ],
        compiler_params=params(),
        name="backward",
    )(*args)


def sum_kernel(
    outp, dxp, dwup, dwq, dwb, small, ro, rd, ga, gb, pk, buf1, pair, buf2, quad, buf3, fin,
    t_s, t_r, loc, s1_s, s1_r, s2_s, s2_r, s3_s, s3_r, z_s, z_r,
):
    z, y, xh, xl, c = place()
    x = xh * 2 + xl
    zpeer = [dev((z + k) % 4, y, x, c) for k in range(4)]
    home = [dev((z + k) % 4, y, c * 2 + xl, xh) for k in range(4)]
    first = [dev(z, (y + k * (1 - c)) % 4, (x + k * c) % 4, c) for k in range(4)]
    second = [dev(z, (y + k * c) % 4, (x + k * (1 - c)) % 4, c) for k in range(4)]
    partner = dev(z, y, x, 1 - c)

    def slot(k1, k2, cc):
        yy = (y + k1 * (1 - cc) + k2 * cc) % 4
        xx = (x + k1 * cc + k2 * (1 - cc)) % 4
        return yy * 8 + xx * 2 + cc

    bar = pltpu.get_barrier_semaphore()
    for to in zpeer[1:] + first[1:] + second[1:] + [partner]:
        pl.semaphore_signal(bar, inc=1, device_id=to, device_id_type=MESH)

    @pl.when(xh != c)
    def _():
        for to in home:
            pl.semaphore_signal(bar, inc=1, device_id=to, device_id_type=MESH)

    pl.semaphore_wait(bar, 10 + 4 * ((xh + c) % 2))

    toks, stays = [], []
    for t, (src, dst) in enumerate(((outp, ro), (dxp, rd))):
        for k in range(4):
            toks.append(rcopy(src.at[(z + k) % 4], dst.at[z], t_s.at[t, k], t_r.at[t, k], home[k]))
        stays.append(pltpu.make_async_copy(src.at[z], dst.at[z], loc.at[t]))
    for i in (1, 2, 3, 5, 6, 7):
        toks[i].start()

    @pl.when(xh != c)
    def _():
        toks[0].start()
        toks[4].start()

    @pl.when(xh == c)
    def _():
        stays[0].start()
        stays[1].start()

    @pl.loop(0, 32)
    def _(p):
        r = pl.ds(pl.multiple_of(p * 32, 32), 32)
        pk[p, :, :128] = dwup[r, :128] + small[p]
        pk[p, :, 128:UP] = dwup[r, 128:]
        pk[p, :, UP:A] = dwq[r, :]
        pk[p, :, A:] = dwb[p]

    order = [(k1, k2) for k1 in (2, 1, 3, 0) for k2 in (2, 1, 3, 0)]
    sends = []
    for k1, k2 in order:
        d = rcopy(pk.at[slot(k1, k2, 1 - c)], buf1.at[k1, k2], s1_s.at[k1, k2], s1_r.at[k1, k2], partner)
        d.start()
        sends.append(d)
    for k1, k2 in order:
        mine = slot(k1, k2, c)
        rcopy(pk.at[mine], buf1.at[k1, k2], s1_s.at[k1, k2], s1_r.at[k1, k2], partner).wait_recv()
        pair[k1, k2] = (pk[mine].astype(F32) + buf1[k1, k2].astype(F32)).astype(BF16)
        if k1:
            d = rcopy(pair.at[k1, k2], buf2.at[4 - k1, k2], s2_s.at[k1, k2], s2_r.at[4 - k1, k2], first[k1])
            d.start()
            sends.append(d)
    for k2 in (2, 1, 3, 0):
        for k1 in range(1, 4):
            rcopy(pair.at[k1, k2], buf2.at[k1, k2], s2_s.at[k1, k2], s2_r.at[k1, k2], partner).wait_recv()
        total = (
            pair[0, k2].astype(F32) + buf2[1, k2].astype(F32) + buf2[2, k2].astype(F32) + buf2[3, k2].astype(F32)
        )
        if k2:
            quad[k2] = total.astype(BF16)
            d = rcopy(quad.at[k2], buf3.at[4 - k2], s3_s.at[k2], s3_r.at[4 - k2], second[k2])
            d.start()
            sends.append(d)
        else:
            fin[...] = total.reshape(4, 8, W)
    for k in range(1, 4):
        rcopy(quad.at[k], buf3.at[k], s3_s.at[k], s3_r.at[k], partner).wait_recv()
    total = fin[...].reshape(32, W) + buf3[1].astype(F32) + buf3[2].astype(F32) + buf3[3].astype(F32)
    fin[...] = total.reshape(4, 8, W)
    gb[...] = total[:, A:]
    zsends = []
    for k in range(1, 4):
        zz = (z + k) % 4
        d = rcopy(fin.at[zz, :, :A], ga.at[z], z_s.at[k], z_r.at[4 - k], zpeer[k])
        d.start()
        zsends.append(d)
    ga[z] = fin[z, :, :A]
    for d in zsends:
        d.wait()
    for i in (1, 2, 3, 5, 6, 7):
        toks[i].wait()

    @pl.when(xh != c)
    def _():
        toks[0].wait()
        toks[4].wait()

    @pl.when(xh == c)
    def _():
        stays[0].wait()
        stays[1].wait()

    for d in sends:
        d.wait_send()


def sum_all(outp, dxp, dwup, dwq, dwb, small):
    dma = pltpu.SemaphoreType.DMA
    sh = jax.ShapeDtypeStruct
    big = pltpu.VMEM((4, 4, 32, W), BF16)
    row = pltpu.VMEM((4, 32, W), BF16)
    tok = sh((4, 128, 768), BF16)
    return pl.pallas_call(
        sum_kernel,
        out_shape=(tok, tok, sh((4, 8, A), F32), sh((32, B), F32)),
        in_specs=[HBM, HBM, VMEM, VMEM, VMEM, VMEM],
        out_specs=(HBM, HBM, VMEM, VMEM),
        scratch_shapes=[
            pltpu.VMEM((32, 32, W), BF16), big, big, big, row, row, pltpu.VMEM((4, 8, W), F32),
            dma((2, 4)), dma((2, 4)), dma((2,)), dma((4, 4)), dma((4, 4)), dma((4, 4)), dma((4, 4)),
            dma((4,)), dma((4,)), dma((4,)), dma((4,)),
        ],
        compiler_params=params(collective_id=3, has_side_effects=True),
        name="sum_weight_grads",
    )(outp, dxp, dwup, dwq, dwb, small)


def permutations():
    j = np.arange(1024)
    nat = 192 * ((j // 8) % 4) + 6 * (j // 32) + j % 8
    s = (np.arange(768)[:, None] == nat[None, :]) & (j % 8 < 6)[None, :]
    i = np.arange(256)
    nat8 = 6 * (i // 8) + i % 8
    s3 = np.zeros((3, 128, 256), bool)
    for h in range(3):
        s3[h, 64:] = ((64 * h + np.arange(64))[:, None] == nat8[None, :]) & (i % 8 < 6)[None, :]
    return jnp.asarray(s, BF16), jnp.asarray(s3, BF16)


def rotary(first_block):
    f = 10000.0 ** (-2.0 * jnp.arange(8, dtype=F32) / 16)
    lane = np.arange(128) % 64
    freq = jnp.where(lane < 16, jnp.tile(f, 16), 0.0)
    pos = (first_block * 128 + 1024 * jnp.arange(4)[:, None] + jnp.arange(128)[None, :]).reshape(512).astype(F32)
    angle = pos[:, None] * freq[None, :]
    sin = jnp.sin(angle)
    return jnp.cos(angle), jnp.where(lane >= 8, sin, 0.0), jnp.where(lane < 8, -sin, 0.0)


def body(
    inputs, qkv_weight, qkv_bias, out_weight, out_bias, up_weight, up_bias, down_weight, down_bias,
    attn_gain, attn_shift, mlp_gain, mlp_shift, cotangent,
):
    z, y, xh, xl, c = place()
    x, g = inputs[0], cotangent[0]
    qkv5 = qkv_weight[0].reshape(6, 3, 4, 3, 64)
    kv_cols = jnp.stack([qkv5[:, 1], qkv5[:, 2]], axis=3).reshape(6, 4, KV)
    q_cols = qkv5[:, 0].reshape(6, 4, 192)
    rows = jnp.concatenate(
        [up_weight[0].reshape(6, 4, UP), kv_cols, q_cols, jnp.zeros((6, 4, 64), BF16)], axis=-1
    ).astype(F32)
    vectors = (qkv_bias, out_bias, up_bias, down_bias, attn_gain, attn_shift, mlp_gain, mlp_shift)
    mine = jnp.concatenate([v[0] for v in vectors] + [jnp.zeros((A - 78,), BF16)]).astype(F32)
    wz = jnp.concatenate(
        [rows.transpose(1, 0, 2), jnp.broadcast_to(mine, (4, 1, A)), jnp.zeros((4, 1, A), F32)], axis=1
    )
    wb = jnp.concatenate([down_weight[0], out_weight[0], jnp.zeros((2, 768), BF16)], axis=0)
    xa, ga, w = gather_all(x, g, wz, wb)
    xa, ga = xa.reshape(512, 768), ga.reshape(512, 768)

    rows = w.reshape(32, 4, 8, W)[:, :, 6, :128].astype(F32)

    def padded(at):
        return jnp.pad(rows[:, :, at : at + 6], ((0, 0), (0, 0), (0, 2))).reshape(1024)

    vec = jnp.stack([padded(54), padded(60), padded(66), padded(72)] + [jnp.zeros((1024,), F32)] * 4)
    whole = rows.transpose(1, 0, 2).reshape(128, 128)
    qb = lax.dynamic_index_in_dim(whole[:, :18].reshape(3, 4, 192), z, 1, False)
    kvb = jnp.stack([qb[1].reshape(3, 64), qb[2].reshape(3, 64)], axis=1).reshape(KV)
    qb = jnp.broadcast_to(jnp.concatenate([kvb, qb[0], jnp.zeros((64,), F32)])[None], (8, 640))
    ub = lax.dynamic_index_in_dim(whole[:, 24:48].reshape(4, UP), z, 0, True)
    ub = jnp.broadcast_to(ub, (8, UP))
    ob = (whole[:, 18:24] + whole[:, 48:54]).reshape(1, 768) * jnp.where(z == 0, 1.0, 0.0)
    ob = jnp.broadcast_to(ob, (8, 768))

    s, s3 = permutations()
    cos, plus, minus = rotary(2 * y + c)
    kv, qd, na, nm, xhat, ow, dw = front(xa, ga, w, s, s3, vec, qb, cos, plus, minus)
    kv_all = gather_kv(kv.reshape(3, 4, 128, 128)).reshape(3, 4096, 128)
    part, dxm, gs_m, dub, dwup, dwd = mlp(nm, ga, w, dw, xhat, vec, ub)
    o, dq, dkv = attention(qd, kv_all)
    dkv = sum_dkv(dkv.reshape(4, 4, 2, 3, 128, 128))
    outp, dxp, dwq, dwb, gs_a, dqb = back(
        o, dq, dkv, na, xhat, ga, w, ow, part, dxm, dwd, s, s3, vec, ob, cos, plus, minus
    )

    here = jnp.where(jnp.arange(4) == z, 1.0, 0.0).astype(F32)
    kvg = dqb[0, :KV].reshape(3, 2, 64)
    qkvg = jnp.stack([dqb[0, KV : KV + 192], kvg[:, 0].reshape(192), kvg[:, 1].reshape(192)])
    qkvg = (qkvg[:, None, :] * here[None, :, None]).reshape(128, 18)
    obg = jnp.sum(g.astype(F32), axis=0).reshape(128, 6)
    ubg = (dub[0:1] * here[:, None]).reshape(128, 24)
    by_dev = jnp.concatenate([qkvg, obg, ubg, obg], axis=1).reshape(4, 32, 54).transpose(1, 0, 2)
    norms = [v.reshape(32, 4, 8)[:, :, :6] for v in (gs_a[0], gs_a[1], gs_m[0], gs_m[1])]
    small = jnp.concatenate([by_dev] + norms + [jnp.zeros((32, 4, 50), F32)], axis=-1)
    small = jnp.pad(small[:, :, None, :], ((0, 0), (0, 0), (6, 1), (0, 0))).reshape(32, 32, 128).astype(BF16)
    ro, rd, grad_a, grad_b = sum_all(
        outp.reshape(4, 128, 768), dxp.reshape(4, 128, 768), dwup, dwq, dwb, small
    )

    xf, gf = x.astype(F32), g.astype(F32)
    outputs = (xf + jnp.sum(ro.astype(F32), axis=0)).astype(BF16)
    dxh = jnp.sum(rd.astype(F32), axis=0)
    cen = xf - jnp.mean(xf, axis=-1, keepdims=True)
    rstd = lax.rsqrt(jnp.mean(cen * cen, axis=-1, keepdims=True) + 1e-5)
    xn = cen * rstd
    dx = rstd * (dxh - jnp.mean(dxh, axis=-1, keepdims=True) - xn * jnp.mean(dxh * xn, axis=-1, keepdims=True))
    input_grad = gf + dx

    up_grad = grad_a[:, :6, :UP].transpose(1, 0, 2).reshape(6, 3072)
    kvg = grad_a[:, :6, UP : UP + KV].reshape(4, 6, 3, 2, 64).transpose(1, 3, 0, 2, 4).reshape(6, 2, 768)
    qg = grad_a[:, :6, UP + KV : UP + KV + 192].transpose(1, 0, 2).reshape(6, 1, 768)
    qkv_grad = jnp.concatenate([qg, kvg], axis=1).reshape(6, 2304)
    tiny = jnp.sum(grad_a[:, 6, :128], axis=0)
    cuts = np.cumsum([0, 18, 6, 24, 6, 6, 6, 6, 6])
    t = [tiny[a:b][None] for a, b in zip(cuts[:-1], cuts[1:])]
    return (
        outputs[None], input_grad[None], qkv_grad[None], t[0], grad_b[24:30][None], t[1], up_grad[None], t[2],
        grad_b[:24][None], t[3], t[4], t[5], t[6], t[7],
    )


def solution(mesh):
    tok = P("fsdp", "ctx", None)
    mat = P(None, ("ctx", "fsdp"), None)
    row = P(None, ("ctx", "fsdp"))
    in_specs = (tok, mat, row, mat, row, mat, row, mat, row, row, row, row, row, tok)
    out_specs = (tok, tok, mat, row, mat, row, mat, row, mat, row, row, row, row, row)
    return jax.shard_map(body, mesh=mesh, in_specs=in_specs, out_specs=out_specs, check_vma=False)
```

```python
import functools

import jax
import jax.numpy as jnp
import numpy as np
from jax import lax
from jax.experimental import pallas as pl
from jax.experimental.pallas import tpu as pltpu
from jax.sharding import PartitionSpec as P

F32 = jnp.float32
BF16 = jnp.bfloat16
MESH = pl.DeviceIdType.MESH
VMEM = pl.BlockSpec(memory_space=pltpu.VMEM)
HBM = pl.BlockSpec(memory_space=pl.ANY)
MIB = 1024 * 1024

QKV, UP = 640, 768
WQ, WM = QKV + 256, 2 * UP
ZW = QKV + UP + 128
OFF = -1e30

def place():
    ctx, fs = lax.axis_index("ctx"), lax.axis_index("fsdp")
    z, y, xh = ctx // 8, (ctx // 2) % 4, ctx % 2
    xl, c = fs // 2, fs % 2
    return z, y, xh, xl, c


def dev(z, y, x, c):
    return (z * 8 + y * 2 + x // 2, (x % 2) * 2 + c)


def rcopy(src, dst, ss, rs, to):
    return pltpu.make_async_remote_copy(
        src_ref=src, dst_ref=dst, send_sem=ss, recv_sem=rs, device_id=to, device_id_type=MESH
    )


def mm(a, b):
    return jnp.dot(a, b, preferred_element_type=F32)


def mm_nt(a, b):
    return lax.dot_general(a, b, (((1,), (1,)), ((), ())), preferred_element_type=F32)


def mm_tn(a, b):
    return lax.dot_general(a, b, (((0,), (0,)), ((), ())), preferred_element_type=F32)


def params(**kw):
    return pltpu.CompilerParams(vmem_limit_bytes=60 * MIB, **kw)


def ids(shape, axis):
    return lax.broadcasted_iota(jnp.int32, shape, axis)


def div(n, d):
    return ((n.astype(F32) + 0.5) * np.float32(1.0 / d)).astype(jnp.int32)


def one_hot(mask):
    return jnp.where(mask, 1.0, 0.0).astype(BF16)


def vector_places(z):
    j = ids((1, 1024), 1)
    real = j % 8 < 6
    norms = [(j // 8 % 4 + 8 * (j // 32), [jnp.where(real, at + j % 8, -1)]) for at in (54, 60, 66, 72)]
    m = ids((1, QKV), 1)
    is_kv = m < 384
    kind = jnp.where(is_kv, jnp.where(m % 128 < 64, 1, 2), 0)
    col = kind * 768 + 192 * z + jnp.where(is_kv, 64 * (m // 128) + m % 64, m - 384)
    own = div(col, 18)
    qkv = ((own % 32) * 8 + own // 32, [jnp.where(m < 576, col - 18 * own, -1)])
    f = ids((1, UP), 1)
    p = div(f, 24)
    up = (p * 8 + z, [24 + f - 24 * p])
    own = div(f, 6)
    r = f - 6 * own
    out = ((own % 32) * 8 + own // 32, [18 + r, 48 + r])
    return norms, qkv, up, out


def lane_hot(lanes, n):
    lane = ids((128, n), 0)
    hit = lane == lanes[0]
    for more in lanes[1:]:
        hit = hit | (lane == more)
    return one_hot(hit)


def spread(packed, where):
    row, lanes = where
    n = row.shape[1]
    t = mm(packed, lane_hot(lanes, n))
    return jnp.sum(jnp.where(ids((256, n), 0) == row, t, 0.0), axis=0, keepdims=True)


def collect(vector, where):
    row, lanes = where
    n = row.shape[1]
    t = jnp.where(ids((256, n), 0) == row, vector, 0.0).astype(BF16)
    return mm_nt(t, lane_hot(lanes, n))


def turn(tile, cos, plus, minus):
    return tile * cos + pltpu.roll(tile, 8, 1) * plus + pltpu.roll(tile, 120, 1) * minus


def layer_kernel(
    x_ref, g_ref, qw_ref, uw_ref, ow_ref, dw_ref, sv_ref, cos_ref, sp_ref, sm_ref,
    ro, rd, zr, dn_out, o8_out,
    xa, ga, wq, wm, zs, zb, cq, cm, s, s3, big, xh, na, nm, vec, kv, qd, dkv, hid, du, part, dxh,
    ow, dw, att, dqkv, outp, dxp, fm, top, tot, acc, delta,
    kb1, kpair, kb2, mb1, mpair, mb2, mquad, mb3, qb1, qpair, qb2, qquad, qb3,
    swap_s, swap_r, loc, tz_s, tz_r, wz_s, wz_r,
    q1_s, q2_s, q3_s, qr_r, qp_r, m1_s, m2_s, m3_s, mr_r, mp_r,
    ky_s, ky_r, kp_s, kp_r, dp_s, dp_r, dy_s, dy_r,
    ma_s, ma_r, mb_s, mb_r, mc_s, mc_r, qa_s, qa_r, qb_s, qb_r, qc_s, qc_r, t_s, t_r, ze_s, ze_r,
):
    z, y, xhi, xl, c = place()
    x = xhi * 2 + xl
    zpeer = [dev((z + k) % 4, y, x, c) for k in range(4)]
    ypeer = [dev(z, (y + k) % 4, x, c) for k in range(4)]
    xpeer = [dev(z, y, (x + k) % 4, c) for k in range(4)]
    home = [dev((z + k) % 4, y, c * 2 + xl, xhi) for k in range(4)]
    first = [dev(z, (y + k * c) % 4, (x + k * (1 - c)) % 4, c) for k in range(4)]
    second = [dev(z, (y + k * (1 - c)) % 4, (x + k * c) % 4, c) for k in range(4)]
    partner = dev(z, y, x, 1 - c)
    swapped = xhi != c

    def slot(k1, k2):
        return (y + k1 * c + k2 * (1 - c)) % 4, (x + k1 * (1 - c) + k2 * c) % 4

    bar = pltpu.get_barrier_semaphore()
    for to in zpeer[1:] + ypeer[1:] + xpeer[1:] + [partner]:
        pl.semaphore_signal(bar, inc=1, device_id=to, device_id_type=MESH)

    @pl.when(swapped)
    def _():
        for to in home:
            pl.semaphore_signal(bar, inc=1, device_id=to, device_id_type=MESH)

    zs[...] = jnp.zeros((4, 8, ZW), F32)
    qw = qw_ref[0].astype(F32)
    uw = uw_ref[0].astype(F32)
    for i in range(4):
        pieces = []
        for h in range(3):
            at = 192 * i + 64 * h
            pieces += [qw[:, 768 + at : 832 + at], qw[:, 1536 + at : 1600 + at]]
        pieces += [qw[:, 192 * i : 192 * i + 192], jnp.zeros((6, 64), F32)]
        zs[i, 0:6, :QKV] = jnp.concatenate(pieces, axis=1)
        zs[i, 0:6, QKV : QKV + UP] = uw[:, UP * i : UP * i + UP]
        zs[i, 0:1, QKV + UP :] = sv_ref[0:1, :]

    pl.semaphore_wait(bar, 10 + 4 * ((xhi + c) % 2))

    zsends = [rcopy(zs.at[(z + k) % 4], zb.at[z], wz_s.at[k], wz_r.at[4 - k], zpeer[k]) for k in range(1, 4)]
    for d in zsends:
        d.start()
    swaps = [rcopy(src, dst.at[z], swap_s.at[t], swap_r.at[t], home[0]) for t, (src, dst) in enumerate(((x_ref, xa), (g_ref, ga)))]

    @pl.when(swapped)
    def _():
        swaps[0].start()
        swaps[1].start()

    @pl.when(xhi == c)
    def _():
        xa[z] = x_ref[...]
        ga[z] = g_ref[...]

    zb[z] = zs[z]
    j = ids((1, 1024), 1)
    nat = jnp.where(j % 8 < 6, 192 * (j // 8 % 4) + 6 * (j // 32) + j % 8, -1)
    s[...] = one_hot(ids((768, 1024), 0) == nat)
    i8 = ids((1, 256), 1)
    nat8 = jnp.where(i8 % 8 < 6, 6 * (i8 // 8) + i8 % 8, -1)
    for h in range(3):
        dim = ids((128, 256), 0)
        s3[h] = one_hot((dim >= 64) & (dim + (64 * h - 64) == nat8))

    for d in zsends:
        d.wait()
    big[0:32, :QKV] = zb[:, :, :QKV].reshape(32, QKV)
    out8 = jnp.concatenate([ow_ref[0].astype(F32), jnp.zeros((2, 768), F32)], axis=0)
    for i in range(3):
        big[8 * i : 8 * i + 8, QKV:WQ] = out8[:, 256 * i : 256 * i + 256]
    big[24:32, QKV:WQ] = jnp.zeros((8, 256), F32)
    for i in range(4):
        big[24 + i : 25 + i, QKV : QKV + 128] = zb[i, 0:1, QKV + UP :]
    cq[...] = big[0:32, :WQ].astype(BF16)
    cm[:, :UP] = zb[:, :, QKV : QKV + UP].reshape(32, UP).astype(BF16)
    cm[:, UP:] = jnp.concatenate([dw_ref[0].astype(F32), jnp.zeros((8, 768), F32)], axis=0).astype(BF16)
    wq[y, x, c] = cq[...]
    wm[y, x, c] = cm[...]

    class Ring:
        def __init__(self, own, arr, s1, s2, s3s, rr, pr):
            self.own, self.arr, self.s1, self.s2, self.s3, self.rr, self.pr, self.sends = own, arr, s1, s2, s3s, rr, pr, []

        def send(self, src, yy, xx, ss, rs, to):
            d = rcopy(src, self.arr.at[yy, xx, c], ss, rs, to)
            d.start()
            self.sends.append(d)

        def begin(self):
            for k in range(1, 4):
                self.send(self.own, y, x, self.s1.at[k], self.rr.at[4 - k, 0], first[k])
            for k in range(1, 4):
                self.send(self.own, y, x, self.s2.at[0, k], self.rr.at[0, 4 - k], second[k])
            self.send(self.own, y, x, self.s3.at[0, 0], self.pr.at[0, 0], partner)

        def arrived(self, k1, k2, rs, cc):
            yy, xx = slot(k1, k2)
            ref = self.arr.at[yy, xx, cc]
            rcopy(ref, ref, self.s3.at[k1, k2], rs, partner).wait_recv()
            return yy, xx

        def forward(self, k1, k2, on):
            yy, xx = self.arrived(k1, k2, self.rr.at[k1, k2], c)
            src = self.arr.at[yy, xx, c]
            if on:
                for k in range(1, 4):
                    self.send(src, yy, xx, self.s2.at[k1, k], self.rr.at[k1, 4 - k], second[k])
            self.send(src, yy, xx, self.s3.at[k1, k2], self.pr.at[k1, k2], partner)

        def finish(self):
            for k1 in range(4):
                for k2 in range(4):
                    yy, xx = (y + k1 * (1 - c) + k2 * c) % 4, (x + k1 * c + k2 * (1 - c)) % 4
                    ref = self.arr.at[yy, xx, 1 - c]
                    rcopy(ref, ref, self.s3.at[k1, k2], self.pr.at[k1, k2], partner).wait_recv()
            for d in self.sends:
                d.wait_send()

    rq = Ring(cq, wq, q1_s, q2_s, q3_s, qr_r, qp_r)
    rm = Ring(cm, wm, m1_s, m2_s, m3_s, mr_r, mp_r)
    rq.begin()

    def spread_tokens(t, arr):
        @pl.when(swapped)
        def _():
            swaps[t].wait()

        ds = [rcopy(arr.at[z], arr.at[z], tz_s.at[t, k], tz_r.at[t, 4 - k], zpeer[k]) for k in range(1, 4)]
        for d in ds:
            d.start()
        return ds

    xtok = spread_tokens(0, xa)
    rm.begin()
    for k1 in range(1, 4):
        rq.forward(k1, 0, True)
    gtok = spread_tokens(1, ga)
    for k1 in range(1, 4):
        rm.forward(k1, 0, True)
    for d in xtok:
        d.wait()

    big[:, :1024] = mm(xa[...].reshape(512, 768), s[...])
    for k2 in range(1, 4):
        for k1 in range(4):
            rq.forward(k1, k2, False)
    real = jnp.where(j % 8 < 6, 1.0, 0.0).astype(F32)
    for i in range(4):
        r = slice(128 * i, 128 * i + 128)
        v = big[r, :1024]
        mean = jnp.sum(v, axis=1, keepdims=True) * (1.0 / 768.0)
        cen = (v - mean) * real
        var = jnp.sum(cen * cen, axis=1, keepdims=True) * (1.0 / 768.0)
        xh[r, :] = cen * lax.rsqrt(var + 1e-5)
    rq.finish()
    packed = wq[:, :, :, 24:32, QKV : QKV + 128].reshape(256, 128)
    norm_at, qkv_at, up_at, out_at = vector_places(z)
    for i in range(4):
        vec[i : i + 1, :] = spread(packed, norm_at[i])
    for i in range(4):
        r = slice(128 * i, 128 * i + 128)
        na[r, :] = (xh[r, :] * vec[0:1, :] + vec[1:2, :]).astype(BF16)
        nm[r, :] = (xh[r, :] * vec[2:3, :] + vec[3:4, :]).astype(BF16)

    qkv = slice(1024, 1024 + QKV)
    wqkv = wq[:, :, :, :, :QKV].reshape(1024, QKV)
    big[:, qkv] = mm(na[...], wqkv) + spread(packed, qkv_at)
    low = ids((128, 128), 1) < 64
    yc = 2 * y + c
    for i in range(4):
        r = slice(128 * i, 128 * i + 128)
        cos, plus, minus = cos_ref[r, :], sp_ref[r, :], sm_ref[r, :]
        kc, kp, km = jnp.where(low, cos, 1.0), jnp.where(low, plus, 0.0), jnp.where(low, minus, 0.0)
        for h in range(3):
            kv[h, i, yc] = turn(big[r, 1024 + 128 * h : 1152 + 128 * h], kc, kp, km).astype(BF16)
        q01 = turn(big[r, 1408:1536], cos, plus, minus).astype(BF16).astype(F32) * 0.125
        q2 = turn(big[r, 1536:1664], cos, plus, minus).astype(BF16).astype(F32) * 0.125
        qd[0, r, :] = jnp.where(low, q01, 0.0).astype(BF16)
        qd[1, r, :] = jnp.where(low, pltpu.roll(q01, 64, 1), 0.0).astype(BF16)
        qd[2, r, :] = jnp.where(low, q2, 0.0).astype(BF16)

    kvsends = []
    for h in range(3):
        mine = kv.at[h, :, yc]
        ds = [rcopy(mine, mine, ky_s.at[h, k], ky_r.at[h, 4 - k], ypeer[k]) for k in range(1, 4)]
        ds.append(rcopy(mine, mine, kp_s.at[h, 0], kp_r.at[h, 0], partner))
        for d in ds:
            d.start()
        kvsends += ds

    def pass_on(h):
        for k in (1, 3, 2):
            there = kv.at[h, :, 2 * ((y + k) % 4) + c]
            rcopy(there, there, ky_s.at[h, k], ky_r.at[h, k], partner).wait_recv()
            d = rcopy(there, there, kp_s.at[h, k], kp_r.at[h, k], partner)
            d.start()
            kvsends.append(d)

    def kv_here(h):
        for k in range(4):
            there = kv.at[h, :, 2 * ((y + k) % 4) + 1 - c]
            rcopy(there, there, kp_s.at[h, k], kp_r.at[h, k], partner).wait_recv()

    for k2 in range(1, 4):
        for k1 in range(4):
            rm.forward(k1, k2, False)
    for d in gtok:
        d.wait()
    out8 = wq[:, :, :, :, QKV:WQ].reshape(32, 32, 256).astype(F32)
    for i in range(3):
        ow[:, 256 * i : 256 * i + 256] = out8[:, 8 * i : 8 * i + 8].reshape(256, 256).astype(BF16)
    g = ga[...].reshape(512, 768)
    dof = mm_nt(g, ow[...]).astype(BF16)
    for h in range(3):
        qd[h, 512:, :] = mm_nt(dof, s3[h]).astype(BF16)
    rm.finish()
    dw[...] = wm[:, :, :, :, UP:].reshape(32, 32, 768).astype(F32)[:, :24].reshape(768, 768).astype(BF16)
    wup = wm[:, :, :, :, :UP].reshape(1024, UP)
    lanes = slice(2048, 2048 + UP)
    big[:, lanes] = mm(nm[...], wup) + spread(packed, up_at)
    pass_on(0)
    for i in range(4):
        r = slice(128 * i, 128 * i + 128)
        u = big[r, lanes]
        cdf = 0.5 * (1.0 + lax.erf(u * np.float32(np.sqrt(0.5))))
        pdf = jnp.exp(-0.5 * u * u) * np.float32(1.0 / np.sqrt(2.0 * np.pi))
        hid[r, :] = (u * cdf).astype(BF16)
        big[r, lanes] = cdf + u * pdf
    part[...] = mm(hid[...], dw[...])
    du[...] = (mm_nt(g, dw[...]) * big[:, lanes]).astype(BF16)
    pass_on(1)
    dn = mm_nt(du[...], wup)
    grads = [
        jnp.sum(dn * xh[...], axis=0, keepdims=True),
        jnp.sum(dn, axis=0, keepdims=True),
        jnp.sum(du[...].astype(F32), axis=0, keepdims=True),
    ]
    dxh[...] = dn * vec[2:3, :]
    small = collect(grads[0], norm_at[2]) + collect(grads[1], norm_at[3]) + collect(grads[2], up_at)
    small += collect(jnp.sum(ga[z].astype(F32), axis=0, keepdims=True), out_at)
    dwd = mm_tn(hid[...], g).reshape(32, 24, 768)
    dwd = jnp.concatenate([dwd, jnp.zeros((32, 8, 768), F32)], axis=1).astype(BF16)
    wm[:, :, :, :, UP:] = dwd.reshape(4, 4, 2, 32, 768)
    wm[:, :, :, :, :UP] = mm_tn(nm[...], du[...]).astype(BF16).reshape(4, 4, 2, 32, UP)
    msend = rcopy(wm.at[:, :, 1 - c], mb1, ma_s.at[0], ma_r.at[0], partner)
    msend.start()
    pass_on(2)

    msends = []

    def m_pairs():
        msend.wait_recv()
        for k in range(1, 4):
            xx = (x + k) % 4
            for yy in range(4):
                mpair[k, yy] = (wm[yy, xx, c].astype(F32) + mb1[yy, xx].astype(F32)).astype(BF16)
            d = rcopy(mpair.at[k], mb2.at[4 - k], mb_s.at[k], mb_r.at[4 - k], xpeer[k])
            d.start()
            msends.append(d)
        for yy in range(4):
            mpair[0, yy] = (wm[yy, x, c].astype(F32) + mb1[yy, x].astype(F32)).astype(BF16)

    def m_quads():
        for k in range(1, 4):
            rcopy(mpair.at[k], mb2.at[k], mb_s.at[k], mb_r.at[k], partner).wait_recv()
        for k in (1, 2, 3, 0):
            yy = (y + k) % 4
            total = mpair[0, yy].astype(F32) + mb2[1, yy].astype(F32) + mb2[2, yy].astype(F32) + mb2[3, yy].astype(F32)
            if k:
                mquad[k] = total.astype(BF16)
                d = rcopy(mquad.at[k], mb3.at[4 - k], mc_s.at[k], mc_r.at[4 - k], ypeer[k])
                d.start()
                msends.append(d)
            else:
                fm[...] = total

    def m_last():
        for k in range(1, 4):
            rcopy(mquad.at[k], mb3.at[k], mc_s.at[k], mc_r.at[k], partner).wait_recv()
        fm[...] += mb3[1].astype(F32) + mb3[2].astype(F32) + mb3[3].astype(F32)

    row = yc * 128 + ids((128, 1024), 0)
    key = ids((128, 1024), 1)

    def rep(a):
        return jnp.concatenate([a] * 8, axis=1)

    def fold(a, f):
        r = a[:, :128]
        for i in range(1, 8):
            r = f(r, a[:, 128 * i : 128 * i + 128])
        return r

    def keys_of(h, j):
        return kv[h, j].reshape(1024, 128)

    def lane_sum(a, f):
        return jnp.broadcast_to(f(a, axis=1, keepdims=True), (512, 128))

    def attend(h, middle):
        top[...] = jnp.full((512, 128), OFF, F32)
        tot[...] = jnp.zeros((512, 128), F32)
        acc[...] = jnp.zeros((512, 128), F32)
        for j in range(4):
            r0, cols = 128 * j, slice(1024 * j, 1024 * j + 1024)
            sc = mm_nt(qd[h, r0:512, :], keys_of(h, j))
            near = jnp.where(key <= row, sc[:128], OFF)
            sc = near if j == 3 else jnp.concatenate([near, sc[128:]], axis=0)
            big[r0:, cols] = sc
            top[r0:, :] = jnp.maximum(top[r0:, :], fold(sc, jnp.maximum))
        top[...] = lane_sum(top[...], jnp.max)
        for j in range(4):
            r0, cols = 128 * j, slice(1024 * j, 1024 * j + 1024)
            p = jnp.exp(big[r0:, cols] - rep(top[r0:, :]))
            big[r0:, cols] = p
            tot[r0:, :] += fold(p, jnp.add)
            acc[r0:, :] += mm(p.astype(BF16), keys_of(h, j))
        inv = 1.0 / lane_sum(tot[...], jnp.sum)
        tot[...] = inv
        o = acc[...] * inv
        delta[...] = lane_sum(o * qd[h, 512:, :].astype(F32), jnp.sum)
        acc[...] = jnp.zeros((512, 128), F32)
        middle()
        for j in range(4):
            r0, cols = 128 * j, slice(1024 * j, 1024 * j + 1024)
            kvj = keys_of(h, j)
            p = big[r0:, cols] * rep(tot[r0:, :])
            dp = mm_nt(qd[h, 512 + r0 :, :], kvj)
            ds = (p * (dp - rep(delta[r0:, :]))).astype(BF16)
            acc[r0:, :] += mm(ds, kvj)
            d = mm_tn(qd[h, r0:512, :], ds) + mm_tn(qd[h, 512 + r0 :, :], p.astype(BF16))
            for i in range(8):
                dkv[h, j, i // 2, i % 2] = d[:, 128 * i : 128 * i + 128].astype(BF16)
        return mm(o.astype(BF16), s3[h]), acc[...] * 0.125

    halves, ysends = [], []

    def dkv_begin(h):
        d = rcopy(dkv.at[h, :, :, 1 - c], kb1.at[h], dp_s.at[h], dp_r.at[h], partner)
        d.start()
        halves.append(d)

    def dkv_pairs(h):
        halves[h].wait_recv()
        for k in (2, 1, 3, 0):
            yy = (y + k) % 4
            for i in range(4):
                kpair[h, k, i] = (dkv[h, i, yy, c].astype(F32) + kb1[h, i, yy].astype(F32)).astype(BF16)
            if k:
                d = rcopy(kpair.at[h, k], kb2.at[h, 4 - k], dy_s.at[h, k], dy_r.at[h, 4 - k], ypeer[k])
                d.start()
                ysends.append(d)

    def back_tile(i, first_lane, tile, keys):
        r = slice(128 * i, 128 * i + 128)
        cos, plus, minus = cos_ref[r, :], -sp_ref[r, :], -sm_ref[r, :]
        if keys:
            cos, plus, minus = jnp.where(low, cos, 1.0), jnp.where(low, plus, 0.0), jnp.where(low, minus, 0.0)
        dqkv[r, first_lane : first_lane + 128] = turn(tile, cos, plus, minus).astype(BF16)

    def dkv_last(h):
        for k in range(1, 4):
            rcopy(kpair.at[h, k], kb2.at[h, k], dy_s.at[h, k], dy_r.at[h, k], partner).wait_recv()
        for i in range(4):
            total = kpair[h, 0, i].astype(F32) + kb2[h, 1, i].astype(F32) + kb2[h, 2, i].astype(F32) + kb2[h, 3, i].astype(F32)
            back_tile(i, 128 * h, total.T, True)

    kv_here(0)
    o0, d0 = attend(0, lambda: None)
    dkv_begin(0)
    m_pairs()
    kv_here(1)
    o1, d1 = attend(1, lambda: dkv_pairs(0))
    dkv_begin(1)
    m_quads()
    kv_here(2)
    o2, d2 = attend(2, lambda: dkv_pairs(1))
    dkv_begin(2)
    m_last()

    att[...] = (o0 + o1 + o2).astype(BF16)
    outs = part[...] + mm(att[...], ow[...]) + spread(packed, out_at) * jnp.where(z == 0, 1.0, 0.0)
    outp[...] = outs.astype(BF16).reshape(4, 128, 768)
    toks = []
    for t, (src, dst) in enumerate(((outp, ro), (dxp, rd))):
        toks.append([rcopy(src.at[(z + k) % 4], dst.at[z], t_s.at[t, k], t_r.at[t, k], home[k]) for k in range(4)])
    stays = [pltpu.make_async_copy(outp.at[z], ro.at[z], loc.at[0]), pltpu.make_async_copy(dxp.at[z], rd.at[z], loc.at[1])]

    def send_back(t):
        for k in range(1, 4):
            toks[t][k].start()

        @pl.when(swapped)
        def _():
            toks[t][0].start()

        @pl.when(xhi == c)
        def _():
            stays[t].start()

    send_back(0)
    dkv_pairs(2)
    dwo = mm_tn(att[...], g).reshape(32, 8, 768)
    for i in range(4):
        r = slice(128 * i, 128 * i + 128)
        back_tile(i, 384, jnp.where(low, d0[r], pltpu.roll(d1[r], 64, 1)), False)
        back_tile(i, 512, jnp.where(low, d2[r], 0.0), False)
    for h in range(3):
        dkv_last(h)
    dqb = jnp.sum(dqkv[...].astype(F32), axis=0, keepdims=True)
    dn = mm_nt(dqkv[...], wqkv)
    small += collect(jnp.sum(dn * xh[...], axis=0, keepdims=True), norm_at[0])
    small += collect(jnp.sum(dn, axis=0, keepdims=True), norm_at[1]) + collect(dqb, qkv_at)
    dx = (dxh[...] + dn * vec[0:1, :]).astype(BF16)
    dwq = mm_tn(na[...], dqkv[...]).astype(BF16)
    wq[:, :, :, :, :QKV] = dwq.reshape(4, 4, 2, 32, QKV)
    last = jnp.concatenate([small.reshape(32, 8, 128), jnp.zeros((32, 8, 128), F32)], axis=2)
    tail = jnp.concatenate([dwo[:, :, :256], dwo[:, :, 256:512], dwo[:, :, 512:], last], axis=1)
    wq[:, :, :, :, QKV:] = tail.astype(BF16).reshape(4, 4, 2, 32, 256)

    def qslot(k1, k2, cc):
        return (y + k1 * (1 - cc) + k2 * cc) % 4, (x + k1 * cc + k2 * (1 - cc)) % 4

    order = [(k1, k2) for k1 in (2, 1, 3, 0) for k2 in (2, 1, 3, 0)]
    qsends = []
    for k1, k2 in order:
        yy, xx = qslot(k1, k2, 1 - c)
        d = rcopy(wq.at[yy, xx, 1 - c], qb1.at[k1, k2], qa_s.at[k1, k2], qa_r.at[k1, k2], partner)
        d.start()
        qsends.append(d)
    dxp[...] = mm_nt(dx, s[...]).astype(BF16).reshape(4, 128, 768)
    send_back(1)
    for k1, k2 in order:
        yy, xx = qslot(k1, k2, c)
        rcopy(wq.at[yy, xx, c], qb1.at[k1, k2], qa_s.at[k1, k2], qa_r.at[k1, k2], partner).wait_recv()
        qpair[k1, k2] = (wq[yy, xx, c].astype(F32) + qb1[k1, k2].astype(F32)).astype(BF16)
        if k1:
            d = rcopy(qpair.at[k1, k2], qb2.at[4 - k1, k2], qb_s.at[k1, k2], qb_r.at[4 - k1, k2], second[k1])
            d.start()
            qsends.append(d)
    for k2 in (2, 1, 3, 0):
        for k1 in range(1, 4):
            rcopy(qpair.at[k1, k2], qb2.at[k1, k2], qb_s.at[k1, k2], qb_r.at[k1, k2], partner).wait_recv()
        total = qpair[0, k2].astype(F32) + qb2[1, k2].astype(F32) + qb2[2, k2].astype(F32) + qb2[3, k2].astype(F32)
        if k2:
            qquad[k2] = total.astype(BF16)
            d = rcopy(qquad.at[k2], qb3.at[4 - k2], qc_s.at[k2], qc_r.at[4 - k2], first[k2])
            d.start()
            qsends.append(d)
    for k in range(1, 4):
        rcopy(qquad.at[k], qb3.at[k], qc_s.at[k], qc_r.at[k], partner).wait_recv()
    total = total + qb3[1].astype(F32) + qb3[2].astype(F32) + qb3[3].astype(F32)
    zs[:, :, :QKV] = total[:, :QKV].reshape(4, 8, QKV)
    zs[:, :, QKV : QKV + UP] = fm[:, :UP].reshape(4, 8, UP)
    for i in range(4):
        zs[i, 0:1, QKV + UP :] = total[24 + i : 25 + i, QKV : QKV + 128]
    zsends = [rcopy(zs.at[(z + k) % 4], zr.at[z], ze_s.at[k], ze_r.at[4 - k], zpeer[k]) for k in range(1, 4)]
    for d in zsends:
        d.start()
    zr[z] = zs[z]
    dn_out[...] = fm[:, UP:]
    o8_out[...] = jnp.concatenate([total[0:8, QKV:], total[8:16, QKV:], total[16:24, QKV:]], axis=1)

    for d in qsends + msends + ysends + halves + kvsends + [msend]:
        d.wait_send()
    for t in range(2):
        for k in range(1, 4):
            toks[t][k].wait()

        @pl.when(swapped)
        def _():
            toks[t][0].wait()

        @pl.when(xhi == c)
        def _():
            stays[t].wait()

    for d in zsends:
        d.wait()


def layer(x, g, qw, uw, ow, dw, sv, cos, plus, minus):
    sh = jax.ShapeDtypeStruct

    def vm(*shape, dtype=BF16):
        return pltpu.VMEM(shape, dtype)

    def sem(*shape):
        return pltpu.SemaphoreType.DMA(shape)

    tok = (4, 128, 768)
    scratch = [
        vm(*tok), vm(*tok), vm(4, 4, 2, 32, WQ), vm(4, 4, 2, 32, WM), vm(4, 8, ZW, dtype=F32), vm(4, 8, ZW, dtype=F32),
        vm(32, WQ), vm(32, WM), vm(768, 1024), vm(3, 128, 256), vm(512, 4096, dtype=F32), vm(512, 1024, dtype=F32),
        vm(512, 1024), vm(512, 1024), vm(8, 1024, dtype=F32), vm(3, 4, 8, 128, 128), vm(3, 1024, 128),
        vm(3, 4, 4, 2, 128, 128), vm(512, 768), vm(512, 768), vm(512, 768, dtype=F32), vm(512, 1024, dtype=F32),
        vm(256, 768), vm(768, 768), vm(512, 256), vm(512, QKV), vm(*tok), vm(*tok), vm(32, WM, dtype=F32),
    ] + [vm(512, 128, dtype=F32)] * 4 + [
        vm(3, 4, 4, 128, 128), vm(3, 4, 4, 128, 128), vm(3, 4, 4, 128, 128),
        vm(4, 4, 32, WM), vm(4, 4, 32, WM), vm(4, 4, 32, WM), vm(4, 32, WM), vm(4, 32, WM),
        vm(4, 4, 32, WQ), vm(4, 4, 32, WQ), vm(4, 4, 32, WQ), vm(4, 32, WQ), vm(4, 32, WQ),
        sem(2), sem(2), sem(2), sem(2, 4), sem(2, 4), sem(4), sem(4),
        sem(4), sem(4, 4), sem(4, 4), sem(4, 4), sem(4, 4), sem(4), sem(4, 4), sem(4, 4), sem(4, 4), sem(4, 4),
        sem(3, 4), sem(3, 4), sem(3, 4), sem(3, 4), sem(3), sem(3), sem(3, 4), sem(3, 4),
        sem(1), sem(1), sem(4), sem(4), sem(4), sem(4), sem(4, 4), sem(4, 4), sem(4, 4), sem(4, 4), sem(4), sem(4),
        sem(2, 4), sem(2, 4), sem(4), sem(4),
    ]
    return pl.pallas_call(
        layer_kernel,
        out_shape=(sh(tok, BF16), sh(tok, BF16), sh((4, 8, ZW), F32), sh((32, 768), F32), sh((8, 768), F32)),
        in_specs=[VMEM] * 10,
        out_specs=(HBM, HBM, VMEM, VMEM, VMEM),
        scratch_shapes=scratch,
        compiler_params=pltpu.CompilerParams(vmem_limit_bytes=63 * MIB, collective_id=0, has_side_effects=True),
        name="layer",
    )(x, g, qw, uw, ow, dw, sv, cos, plus, minus)


CUTS = (0, 18, 24, 48, 54, 60, 66, 72, 78)


def finish_kernel(x_ref, g_ref, ro, rd, zr, dn, o8, *outs):
    out, dx_out, qkv, up, out_w, down = outs[:6]
    xf = x_ref[...].astype(F32)
    total = ro[0].astype(F32) + ro[1].astype(F32) + ro[2].astype(F32) + ro[3].astype(F32)
    out[0] = (xf + total).astype(BF16)
    dxh = rd[0].astype(F32) + rd[1].astype(F32) + rd[2].astype(F32) + rd[3].astype(F32)
    cen = xf - jnp.mean(xf, axis=1, keepdims=True)
    rstd = lax.rsqrt(jnp.mean(cen * cen, axis=1, keepdims=True) + 1e-5)
    xn = cen * rstd
    mean, along = jnp.mean(dxh, axis=1, keepdims=True), jnp.mean(dxh * xn, axis=1, keepdims=True)
    dx_out[0] = g_ref[...].astype(F32) + rstd * (dxh - mean - xn * along)
    pieces = [zr[i, 0:6, 384:576] for i in range(4)]
    pieces += [zr[i, 0:6, 128 * h : 128 * h + 64] for i in range(4) for h in range(3)]
    pieces += [zr[i, 0:6, 128 * h + 64 : 128 * h + 128] for i in range(4) for h in range(3)]
    qkv[0] = jnp.concatenate(pieces, axis=1)
    up[0] = jnp.concatenate([zr[i, 0:6, QKV : QKV + UP] for i in range(4)], axis=1)
    out_w[0] = o8[0:6, :]
    down[0] = dn[0:24, :]
    rows = sum(zr[i, 0:1, QKV + UP :] for i in range(4))
    for ref, a, b in zip(outs[6:], CUTS[:-1], CUTS[1:]):
        ref[...] = rows[:, a:b]


def finish(*args):
    def sh(*shape, dtype=F32):
        return jax.ShapeDtypeStruct(shape, dtype)

    shapes = [sh(1, 128, 768, dtype=BF16), sh(1, 128, 768), sh(1, 6, 2304), sh(1, 6, 3072), sh(1, 6, 768), sh(1, 24, 768)]
    shapes += [sh(1, b - a) for a, b in zip(CUTS[:-1], CUTS[1:])]
    return pl.pallas_call(
        finish_kernel,
        out_shape=tuple(shapes),
        in_specs=[VMEM] * 7,
        out_specs=(VMEM,) * 14,
        compiler_params=params(),
        name="finish",
    )(*args)


def rotary(first_block):
    f = 10000.0 ** (-2.0 * jnp.arange(8, dtype=F32) / 16)
    lane = np.arange(128) % 64
    freq = jnp.where(lane < 16, jnp.tile(f, 16), 0.0)
    pos = (first_block * 128 + 1024 * jnp.arange(4)[:, None] + jnp.arange(128)[None, :]).reshape(512).astype(F32)
    angle = pos[:, None] * freq[None, :]
    sin = jnp.sin(angle)
    return jnp.cos(angle), jnp.where(lane >= 8, sin, 0.0), jnp.where(lane < 8, -sin, 0.0)


def body(
    inputs, qkv_weight, qkv_bias, out_weight, out_bias, up_weight, up_bias, down_weight, down_bias,
    attn_gain, attn_shift, mlp_gain, mlp_shift, cotangent,
):
    z, y, xh, xl, c = place()
    x, g = inputs[0], cotangent[0]
    vectors = (qkv_bias, out_bias, up_bias, down_bias, attn_gain, attn_shift, mlp_gain, mlp_shift)
    sv = jnp.concatenate([v[0] for v in vectors] + [jnp.zeros((50,), BF16)]).astype(F32)
    sv = jnp.broadcast_to(sv[None], (8, 128))
    cos, plus, minus = rotary(2 * y + c)
    ro, rd, zr, dn, o8 = layer(x, g, qkv_weight, up_weight, out_weight, down_weight, sv, cos, plus, minus)
    out, dx, qkv, up, ow, dw, *t = finish(x, g, ro, rd, zr, dn, o8)
    return out, dx, qkv, t[0], ow, t[1], up, t[2], dw, t[3], t[4], t[5], t[6], t[7]


def solution(mesh):
    tok = P("fsdp", "ctx", None)
    mat = P(None, ("ctx", "fsdp"), None)
    row = P(None, ("ctx", "fsdp"))
    in_specs = (tok, mat, row, mat, row, mat, row, mat, row, row, row, row, row, tok)
    out_specs = (tok, tok, mat, row, mat, row, mat, row, mat, row, row, row, row, row)
    return jax.shard_map(body, mesh=mesh, in_specs=in_specs, out_specs=out_specs, check_vma=False)
```

```python
import functools

import jax
import jax.numpy as jnp
import numpy as np
from jax import lax
from jax.experimental import pallas as pl
from jax.experimental.pallas import tpu as pltpu
from jax.sharding import PartitionSpec as P

F32 = jnp.float32
BF16 = jnp.bfloat16
MESH = pl.DeviceIdType.MESH
VMEM = pl.BlockSpec(memory_space=pltpu.VMEM)
HBM = pl.BlockSpec(memory_space=pl.ANY)
MIB = 1024 * 1024

QKV, UP = 640, 768
ZW = QKV + UP + 128
OFF = -1e30

def place():
    ctx, fs = lax.axis_index("ctx"), lax.axis_index("fsdp")
    z, y, xh = ctx // 8, (ctx // 2) % 4, ctx % 2
    xl, c = fs // 2, fs % 2
    return z, y, xh, xl, c


def dev(z, y, x, c):
    return (z * 8 + y * 2 + x // 2, (x % 2) * 2 + c)


def rcopy(src, dst, ss, rs, to):
    return pltpu.make_async_remote_copy(
        src_ref=src, dst_ref=dst, send_sem=ss, recv_sem=rs, device_id=to, device_id_type=MESH
    )


def mm(a, b):
    return jnp.dot(a, b, preferred_element_type=F32)


def mm_nt(a, b):
    return lax.dot_general(a, b, (((1,), (1,)), ((), ())), preferred_element_type=F32)


def mm_tn(a, b):
    return lax.dot_general(a, b, (((0,), (0,)), ((), ())), preferred_element_type=F32)


def params(**kw):
    return pltpu.CompilerParams(vmem_limit_bytes=60 * MIB, **kw)


def ids(shape, axis):
    return lax.broadcasted_iota(jnp.int32, shape, axis)


def div(n, d):
    return ((n.astype(F32) + 0.5) * np.float32(1.0 / d)).astype(jnp.int32)


def one_hot(mask):
    return jnp.where(mask, 1.0, 0.0).astype(BF16)


def owner(j):
    p = div(j, 24)
    return p, j - 24 * p


def vector_places(z):
    j = ids((1, 768), 1)
    p, of = owner(j)
    norms = [(8 * p + div(of, 6), [at + of - 6 * div(of, 6)]) for at in (54, 60, 66, 72)]
    m = ids((1, QKV), 1)
    is_kv = m < 384
    kind = jnp.where(is_kv, jnp.where(m % 128 < 64, 1, 2), 0)
    col = kind * 768 + 192 * z + jnp.where(is_kv, 64 * (m // 128) + m % 64, m - 384)
    own = div(col, 18)
    qkv = ((own % 32) * 8 + own // 32, [jnp.where(m < 576, col - 18 * own, -1)])
    f = ids((1, UP), 1)
    p = div(f, 24)
    up = (p * 8 + z, [24 + f - 24 * p])
    own = div(f, 6)
    r = f - 6 * own
    out = ((own % 32) * 8 + own // 32, [18 + r, 48 + r])
    return norms, qkv, up, out


def lane_hot(lanes, n):
    lane = ids((128, n), 0)
    hit = lane == lanes[0]
    for more in lanes[1:]:
        hit = hit | (lane == more)
    return one_hot(hit)


def spread(packed, where):
    row, lanes = where
    n = row.shape[1]
    t = mm(packed, lane_hot(lanes, n))
    return jnp.sum(jnp.where(ids((256, n), 0) == row, t, 0.0), axis=0, keepdims=True)


def collect(vector, where):
    row, lanes = where
    n = row.shape[1]
    t = jnp.where(ids((256, n), 0) == row, vector, 0.0).astype(BF16)
    return mm_nt(t, lane_hot(lanes, n))


def turn(tile, cos, plus, minus):
    return tile * cos + pltpu.roll(tile, 8, 1) * plus + pltpu.roll(tile, 120, 1) * minus


def layer_kernel(
    x_ref, g_ref, qw_ref, uw_ref, ow_ref, dw_ref, v0, v1, v2, v3, v4, v5, v6, v7,
    ro, rd, zr, dn_out, o8_out,
    xa, ga, wq, wm, zs, zb, cq, cm, s, s3, big, xh, na, nm, vec, kv, qd, dkv, hid, du, part, dxh,
    ow, dw, wn, att, dqkv, outp, obuf, dxp, fm, cos_ref, sp_ref, sm_ref, top, tot, acc, delta,
    kb1, kpair, kb2, mb1, mpair, mb2, mquad, mb3, qb1, qpair, qb2, qquad, qb3,
    swap_s, swap_r, loc, tz_s, tz_r, wz_s, wz_r,
    q1_s, q2_s, q3_s, qr_r, qp_r, m1_s, m2_s, m3_s, mr_r, mp_r,
    ky_s, ky_r, kp_s, kp_r, dp_s, dp_r, dy_s, dy_r,
    ma_s, ma_r, mb_s, mb_r, mc_s, mc_r, qa_s, qa_r, qb_s, qb_r, qc_s, qc_r, t_s, t_r, o_s, o_r, ze_s, ze_r,
):
    z, y, xhi, xl, c = place()
    x = xhi * 2 + xl
    zpeer = [dev((z + k) % 4, y, x, c) for k in range(4)]
    ypeer = [dev(z, (y + k) % 4, x, c) for k in range(4)]
    xpeer = [dev(z, y, (x + k) % 4, c) for k in range(4)]
    home = [dev((z + k) % 4, y, c * 2 + xl, xhi) for k in range(4)]
    first = [dev(z, (y + k * c) % 4, (x + k * (1 - c)) % 4, c) for k in range(4)]
    second = [dev(z, (y + k * (1 - c)) % 4, (x + k * c) % 4, c) for k in range(4)]
    partner = dev(z, y, x, 1 - c)
    swapped = xhi != c

    def q_slot(k1, k2, cc):
        return (y + k1 * cc + k2 * (1 - cc)) % 4, (x + k1 * (1 - cc) + k2 * cc) % 4

    def m_slot(k1, k2, cc):
        return (y + k1) % 4, (x + k2) % 4

    bar = pltpu.get_barrier_semaphore()
    for to in zpeer[1:] + ypeer[1:] + xpeer[1:] + [partner]:
        pl.semaphore_signal(bar, inc=1, device_id=to, device_id_type=MESH)

    @pl.when(swapped)
    def _():
        for to in home:
            pl.semaphore_signal(bar, inc=1, device_id=to, device_id_type=MESH)

    zs[...] = jnp.zeros((4, 8, ZW), F32)
    qw = qw_ref[0].astype(F32)
    uw = uw_ref[0].astype(F32)
    vectors = [v[...].astype(F32) for v in (v0, v1, v2, v3, v4, v5, v6, v7)]
    vectors = jnp.concatenate(vectors + [jnp.zeros((1, 50), F32)], axis=1)
    for i in range(4):
        pieces = []
        for h in range(3):
            at = 192 * i + 64 * h
            pieces += [qw[:, 768 + at : 832 + at], qw[:, 1536 + at : 1600 + at]]
        pieces += [qw[:, 192 * i : 192 * i + 192], jnp.zeros((6, 64), F32)]
        zs[i, 0:6, :QKV] = jnp.concatenate(pieces, axis=1)
        zs[i, 0:6, QKV : QKV + UP] = uw[:, UP * i : UP * i + UP]
        zs[i, 0:1, QKV + UP :] = vectors

    pl.semaphore_wait(bar, 10 + 4 * ((xhi + c) % 2))

    zsends = [rcopy(zs.at[(z + k) % 4], zb.at[z], wz_s.at[k], wz_r.at[4 - k], zpeer[k]) for k in range(1, 4)]
    for d in zsends:
        d.start()
    swaps = [rcopy(src, dst.at[z], swap_s.at[t], swap_r.at[t], home[0]) for t, (src, dst) in enumerate(((x_ref, xa), (g_ref, ga)))]

    @pl.when(swapped)
    def _():
        swaps[0].start()
        swaps[1].start()

    @pl.when(xhi == c)
    def _():
        xa[z] = x_ref[...]
        ga[z] = g_ref[...]

    zb[z] = zs[z]
    p, of = owner(ids((1, 768), 1))
    nat = 192 * div(of, 6) + 6 * p + of - 6 * div(of, 6)
    s[...] = one_hot(ids((768, 768), 0) == nat)
    i8 = ids((1, 256), 1)
    nat8 = jnp.where(i8 % 8 < 6, 6 * (i8 // 8) + i8 % 8, -1)
    for h in range(3):
        dim = ids((128, 256), 0)
        s3[h] = one_hot((dim >= 64) & (dim + (64 * h - 64) == nat8))

    for d in zsends:
        d.wait()
    rows = [zb[i, 0:6, :] for i in range(4)]
    rows = jnp.concatenate(rows, axis=0)
    out8 = ow_ref[0].astype(F32)
    tails = [out8[i : i + 1, 640:] for i in range(6)]
    row6 = jnp.concatenate(tails[:5], axis=1)
    row7 = jnp.concatenate(tails[5:] + [zb[i, 0:1, QKV + UP :] for i in range(4)], axis=1)
    cq[...] = jnp.concatenate([rows[:, :QKV], out8[:, :640], row6, row7], axis=0).astype(BF16)
    cm[...] = jnp.concatenate([rows[:, QKV : QKV + UP], dw_ref[0].astype(F32)], axis=0).astype(BF16)
    wq[y, x, c] = cq[...]
    wm[y, x, c] = cm[...]

    class Ring:
        def __init__(self, own, arr, slot, one, two, s1, s2, s3s, rr, pr):
            self.slot, self.one, self.two = slot, one, two
            self.own, self.arr, self.s1, self.s2, self.s3, self.rr, self.pr, self.sends = own, arr, s1, s2, s3s, rr, pr, []

        def send(self, src, yy, xx, ss, rs, to):
            d = rcopy(src, self.arr.at[yy, xx, c], ss, rs, to)
            d.start()
            self.sends.append(d)

        def begin(self):
            for k in range(1, 4):
                self.send(self.own, y, x, self.s1.at[k], self.rr.at[4 - k, 0], self.one[k])
            for k in range(1, 4):
                self.send(self.own, y, x, self.s2.at[0, k], self.rr.at[0, 4 - k], self.two[k])
            self.send(self.own, y, x, self.s3.at[0, 0], self.pr.at[0, 0], partner)

        def arrived(self, k1, k2, rs, cc):
            yy, xx = self.slot(k1, k2, cc)
            ref = self.arr.at[yy, xx, cc]
            rcopy(ref, ref, self.s3.at[k1, k2], rs, partner).wait_recv()
            return yy, xx

        def forward(self, k1, k2, on):
            yy, xx = self.arrived(k1, k2, self.rr.at[k1, k2], c)
            src = self.arr.at[yy, xx, c]
            if on:
                for k in range(1, 4):
                    self.send(src, yy, xx, self.s2.at[k1, k], self.rr.at[k1, 4 - k], self.two[k])
            self.send(src, yy, xx, self.s3.at[k1, k2], self.pr.at[k1, k2], partner)

        def finish(self):
            for k1 in range(4):
                for k2 in range(4):
                    yy, xx = self.slot(k1, k2, 1 - c)
                    ref = self.arr.at[yy, xx, 1 - c]
                    rcopy(ref, ref, self.s3.at[k1, k2], self.pr.at[k1, k2], partner).wait_recv()
            for d in self.sends:
                d.wait_send()

    rq = Ring(cq, wq, q_slot, first, second, q1_s, q2_s, q3_s, qr_r, qp_r)
    rm = Ring(cm, wm, m_slot, ypeer, xpeer, m1_s, m2_s, m3_s, mr_r, mp_r)
    rq.begin()

    def spread_tokens(t, arr):
        @pl.when(swapped)
        def _():
            swaps[t].wait()

        ds = [rcopy(arr.at[z], arr.at[z], tz_s.at[t, k], tz_r.at[t, 4 - k], zpeer[k]) for k in range(1, 4)]
        for d in ds:
            d.start()
        return ds

    xtok = spread_tokens(0, xa)
    rm.begin()
    for k1 in range(1, 4):
        rq.forward(k1, 0, True)
    gtok = spread_tokens(1, ga)
    for k1 in range(1, 4):
        rm.forward(k1, 0, True)

    lane = ids((128, 128), 1) % 64
    freq = jnp.exp((lane % 8).astype(F32) * np.float32(-2.0 / 16 * np.log(10000.0)))
    freq = jnp.where(lane < 16, freq, 0.0)
    yc = 2 * y + c
    for i in range(4):
        r = slice(128 * i, 128 * i + 128)
        angle = ((8 * i + yc) * 128 + ids((128, 128), 0)).astype(F32) * freq
        sin = jnp.sin(angle)
        cos_ref[r, :] = jnp.cos(angle)
        sp_ref[r, :] = jnp.where(lane >= 8, sin, 0.0)
        sm_ref[r, :] = jnp.where(lane < 8, -sin, 0.0)
    for d in xtok:
        d.wait()
    big[:, :768] = mm(xa[...].reshape(512, 768), s[...])
    for k2 in range(1, 4):
        for k1 in range(4):
            rq.forward(k1, k2, False)
    for i in range(4):
        r = slice(128 * i, 128 * i + 128)
        v = big[r, :768]
        cen = v - jnp.sum(v, axis=1, keepdims=True) * (1.0 / 768.0)
        var = jnp.sum(cen * cen, axis=1, keepdims=True) * (1.0 / 768.0)
        xh[r, :] = cen * lax.rsqrt(var + 1e-5)
    rq.finish()
    rest = wq[...].reshape(32, 32, QKV).astype(F32)
    wqkv = rest[:, :24].reshape(768, QKV).astype(BF16)
    rest = rest[:, 24:]
    packed = [rest[:, 7:8, 128 + 128 * i : 256 + 128 * i] for i in range(4)] + [jnp.zeros((32, 4, 128), F32)]
    packed = jnp.concatenate(packed, axis=1).reshape(256, 128).astype(BF16)
    norm_at, qkv_at, up_at, out_at = vector_places(z)
    for i in range(4):
        vec[i : i + 1, :] = spread(packed, norm_at[i])
    for i in range(4):
        r = slice(128 * i, 128 * i + 128)
        na[r, :] = (xh[r, :] * vec[0:1, :] + vec[1:2, :]).astype(BF16)
        nm[r, :] = (xh[r, :] * vec[2:3, :] + vec[3:4, :]).astype(BF16)

    wn[...] = wqkv
    big[:, 1024 : 1024 + QKV] = mm(na[...], wqkv) + spread(packed, qkv_at)
    low = ids((128, 128), 1) < 64
    for i in range(4):
        r = slice(128 * i, 128 * i + 128)
        cos, plus, minus = cos_ref[r, :], sp_ref[r, :], sm_ref[r, :]
        kc, kp, km = jnp.where(low, cos, 1.0), jnp.where(low, plus, 0.0), jnp.where(low, minus, 0.0)
        for h in range(3):
            kv[h, i, yc] = turn(big[r, 1024 + 128 * h : 1152 + 128 * h], kc, kp, km).astype(BF16)
        q01 = turn(big[r, 1408:1536], cos, plus, minus).astype(BF16).astype(F32) * 0.125
        q2 = turn(big[r, 1536:1664], cos, plus, minus).astype(BF16).astype(F32) * 0.125
        qd[0, r, :] = jnp.where(low, q01, 0.0).astype(BF16)
        qd[1, r, :] = jnp.where(low, pltpu.roll(q01, 64, 1), 0.0).astype(BF16)
        qd[2, r, :] = jnp.where(low, q2, 0.0).astype(BF16)

    kvsends = []
    for h in range(3):
        mine = kv.at[h, :, yc]
        ds = [rcopy(mine, mine, ky_s.at[h, k], ky_r.at[h, 4 - k], ypeer[k]) for k in range(1, 4)]
        ds.append(rcopy(mine, mine, kp_s.at[h, 0], kp_r.at[h, 0], partner))
        for d in ds:
            d.start()
        kvsends += ds

    def pass_on(h):
        for k in (1, 3, 2):
            there = kv.at[h, :, 2 * ((y + k) % 4) + c]
            rcopy(there, there, ky_s.at[h, k], ky_r.at[h, k], partner).wait_recv()
            d = rcopy(there, there, kp_s.at[h, k], kp_r.at[h, k], partner)
            d.start()
            kvsends.append(d)

    def kv_here(h):
        for k in range(4):
            there = kv.at[h, :, 2 * ((y + k) % 4) + 1 - c]
            rcopy(there, there, kp_s.at[h, k], kp_r.at[h, k], partner).wait_recv()

    for k2 in range(1, 4):
        for k1 in range(4):
            rm.forward(k1, k2, False)
    for d in gtok:
        d.wait()
    tails = [rest[:, 6:7, 128 * i : 128 * i + 128] for i in range(5)] + [rest[:, 7:8, :128], jnp.zeros((32, 2, 128), F32)]
    ow[:, :640] = rest.reshape(256, 640).astype(BF16)
    ow[:, 640:] = jnp.concatenate(tails, axis=1).reshape(256, 128).astype(BF16)
    g = ga[...].reshape(512, 768)
    dof = mm_nt(g, ow[...]).astype(BF16)
    for h in range(3):
        qd[h, 512:, :] = mm_nt(dof, s3[h]).astype(BF16)
    pass_on(0)
    rm.finish()

    msends = []

    def m_pairs():
        msend.wait_recv()
        for k in range(1, 4):
            xx = (x + k) % 4
            for yy in range(4):
                mpair[k, yy] = (wm[yy, xx, c].astype(F32) + mb1[yy, xx].astype(F32)).astype(BF16)
            d = rcopy(mpair.at[k], mb2.at[4 - k], mb_s.at[k], mb_r.at[4 - k], xpeer[k])
            d.start()
            msends.append(d)
        for yy in range(4):
            mpair[0, yy] = (wm[yy, x, c].astype(F32) + mb1[yy, x].astype(F32)).astype(BF16)

    def m_quads():
        for k in range(1, 4):
            rcopy(mpair.at[k], mb2.at[k], mb_s.at[k], mb_r.at[k], partner).wait_recv()
        for k in (1, 2, 3, 0):
            yy = (y + k) % 4
            total = mpair[0, yy].astype(F32) + mb2[1, yy].astype(F32) + mb2[2, yy].astype(F32) + mb2[3, yy].astype(F32)
            if k:
                mquad[k] = total.astype(BF16)
                d = rcopy(mquad.at[k], mb3.at[4 - k], mc_s.at[k], mc_r.at[4 - k], ypeer[k])
                d.start()
                msends.append(d)
            else:
                fm[...] = total

    def m_last():
        for k in range(1, 4):
            rcopy(mquad.at[k], mb3.at[k], mc_s.at[k], mc_r.at[k], partner).wait_recv()
        fm[...] += mb3[1].astype(F32) + mb3[2].astype(F32) + mb3[3].astype(F32)

    row = yc * 128 + ids((128, 1024), 0)
    key = ids((128, 1024), 1)

    def rep(a):
        return jnp.concatenate([a] * 8, axis=1)

    def fold(a, f):
        r = a[:, :128]
        for i in range(1, 8):
            r = f(r, a[:, 128 * i : 128 * i + 128])
        return r

    def keys_of(h, j):
        return kv[h, j].reshape(1024, 128)

    def lane_sum(a, f):
        return jnp.broadcast_to(f(a, axis=1, keepdims=True), (512, 128))

    def attend(h, middle):
        top[...] = jnp.full((512, 128), OFF, F32)
        tot[...] = jnp.zeros((512, 128), F32)
        acc[...] = jnp.zeros((512, 128), F32)
        for j in range(4):
            r0, cols = 128 * j, slice(1024 * j, 1024 * j + 1024)
            sc = mm_nt(qd[h, r0:512, :], keys_of(h, j))
            near = jnp.where(key <= row, sc[:128], OFF)
            sc = near if j == 3 else jnp.concatenate([near, sc[128:]], axis=0)
            big[r0:, cols] = sc
            top[r0:, :] = jnp.maximum(top[r0:, :], fold(sc, jnp.maximum))
        top[...] = lane_sum(top[...], jnp.max)
        for j in range(4):
            r0, cols = 128 * j, slice(1024 * j, 1024 * j + 1024)
            p = jnp.exp(big[r0:, cols] - rep(top[r0:, :]))
            big[r0:, cols] = p
            tot[r0:, :] += fold(p, jnp.add)
            acc[r0:, :] += mm(p.astype(BF16), keys_of(h, j))
        inv = 1.0 / lane_sum(tot[...], jnp.sum)
        tot[...] = inv
        o = acc[...] * inv
        delta[...] = lane_sum(o * qd[h, 512:, :].astype(F32), jnp.sum)
        acc[...] = jnp.zeros((512, 128), F32)
        middle()
        for j in range(4):
            r0, cols = 128 * j, slice(1024 * j, 1024 * j + 1024)
            kvj = keys_of(h, j)
            p = big[r0:, cols] * rep(tot[r0:, :])
            dp = mm_nt(qd[h, 512 + r0 :, :], kvj)
            ds = (p * (dp - rep(delta[r0:, :]))).astype(BF16)
            acc[r0:, :] += mm(ds, kvj)
            d = mm_tn(qd[h, r0:512, :], ds) + mm_tn(qd[h, 512 + r0 :, :], p.astype(BF16))
            for i in range(8):
                dkv[h, j, i // 2, i % 2] = d[:, 128 * i : 128 * i + 128].astype(BF16)
        return mm(o.astype(BF16), s3[h]), acc[...] * 0.125

    halves, ysends = [], []

    def dkv_begin(h):
        d = rcopy(dkv.at[h, :, :, 1 - c], kb1.at[h], dp_s.at[h], dp_r.at[h], partner)
        d.start()
        halves.append(d)

    def dkv_pairs(h):
        halves[h].wait_recv()
        for k in (2, 1, 3, 0):
            yy = (y + k) % 4
            for i in range(4):
                kpair[h, k, i] = (dkv[h, i, yy, c].astype(F32) + kb1[h, i, yy].astype(F32)).astype(BF16)
            if k:
                d = rcopy(kpair.at[h, k], kb2.at[h, 4 - k], dy_s.at[h, k], dy_r.at[h, 4 - k], ypeer[k])
                d.start()
                ysends.append(d)

    def back_tile(i, first_lane, tile, keys):
        r = slice(128 * i, 128 * i + 128)
        cos, plus, minus = cos_ref[r, :], -sp_ref[r, :], -sm_ref[r, :]
        if keys:
            cos, plus, minus = jnp.where(low, cos, 1.0), jnp.where(low, plus, 0.0), jnp.where(low, minus, 0.0)
        dqkv[r, first_lane : first_lane + 128] = turn(tile, cos, plus, minus).astype(BF16)

    def dkv_last(h):
        for k in range(1, 4):
            rcopy(kpair.at[h, k], kb2.at[h, k], dy_s.at[h, k], dy_r.at[h, k], partner).wait_recv()
        for i in range(4):
            total = kpair[h, 0, i].astype(F32) + kb2[h, 1, i].astype(F32) + kb2[h, 2, i].astype(F32) + kb2[h, 3, i].astype(F32)
            back_tile(i, 128 * h, total.T, True)

    kv_here(0)
    o0, d0 = attend(0, lambda: None)
    dkv_begin(0)
    pass_on(1)

    w48 = wm[...].reshape(32, 48, 768).astype(F32)
    dw[...] = w48[:, 24:].reshape(768, 768).astype(BF16)
    wup = w48[:, :24].reshape(768, UP).astype(BF16)
    lanes = slice(2048, 2048 + UP)
    big[:, lanes] = mm(nm[...], wup) + spread(packed, up_at)
    for i in range(4):
        r = slice(128 * i, 128 * i + 128)
        u = big[r, lanes]
        cdf = 0.5 * (1.0 + lax.erf(u * np.float32(np.sqrt(0.5))))
        pdf = jnp.exp(-0.5 * u * u) * np.float32(1.0 / np.sqrt(2.0 * np.pi))
        hid[r, :] = (u * cdf).astype(BF16)
        big[r, lanes] = cdf + u * pdf
    part[...] = mm(hid[...], dw[...])
    du[...] = (mm_nt(g, dw[...]) * big[:, lanes]).astype(BF16)
    dn = mm_nt(du[...], wup)
    grads = [
        jnp.sum(dn * xh[...], axis=0, keepdims=True),
        jnp.sum(dn, axis=0, keepdims=True),
        jnp.sum(du[...].astype(F32), axis=0, keepdims=True),
    ]
    dxh[...] = dn * vec[2:3, :]
    small = collect(grads[0], norm_at[2]) + collect(grads[1], norm_at[3]) + collect(grads[2], up_at)
    small += collect(jnp.sum(ga[z].astype(F32), axis=0, keepdims=True), out_at)
    dwu = mm_tn(nm[...], du[...]).reshape(32, 24, 768)
    dwd = mm_tn(hid[...], g).reshape(32, 24, 768)
    wm[...] = jnp.concatenate([dwu, dwd], axis=1).astype(BF16).reshape(4, 4, 2, 48, 768)
    msend = rcopy(wm.at[:, :, 1 - c], mb1, ma_s.at[0], ma_r.at[0], partner)
    msend.start()
    pass_on(2)
    dkv_pairs(0)
    kv_here(1)
    o1, d1 = attend(1, m_pairs)
    dkv_begin(1)
    kv_here(2)
    o2, d2 = attend(2, lambda: dkv_pairs(1))
    dkv_begin(2)

    att[...] = (o0 + o1 + o2).astype(BF16)
    outs = part[...] + mm(att[...], ow[...]) + spread(packed, out_at) * jnp.where(z == 0, 1.0, 0.0)
    outp[...] = outs.astype(BF16).reshape(4, 128, 768)
    osends = [rcopy(outp.at[(z + k) % 4], obuf.at[z], o_s.at[k], o_r.at[4 - k], zpeer[k]) for k in range(1, 4)]
    for d in osends:
        d.start()
    dkv_pairs(2)
    dwo = mm_tn(att[...], g).reshape(32, 8, 768)
    for i in range(4):
        r = slice(128 * i, 128 * i + 128)
        back_tile(i, 384, jnp.where(low, d0[r], pltpu.roll(d1[r], 64, 1)), False)
        back_tile(i, 512, jnp.where(low, d2[r], 0.0), False)
    dkv_last(0)
    for d in osends:
        d.wait()
    obuf[z] = outp[z]
    outs = obuf[0].astype(F32) + obuf[1].astype(F32) + obuf[2].astype(F32) + obuf[3].astype(F32)
    outp[0] = (xa[z].astype(F32) + outs).astype(BF16)
    out_swap = rcopy(outp.at[0], ro, o_s.at[0], o_r.at[0], home[0])
    out_stay = pltpu.make_async_copy(outp.at[0], ro, loc.at[0])

    @pl.when(swapped)
    def _():
        out_swap.start()

    @pl.when(xhi == c)
    def _():
        out_stay.start()

    m_quads()
    for h in (1, 2):
        dkv_last(h)
    dqb = jnp.sum(dqkv[...].astype(F32), axis=0, keepdims=True)
    dn = mm_nt(dqkv[...], wn[...])
    small += collect(jnp.sum(dn * xh[...], axis=0, keepdims=True), norm_at[0])
    small += collect(jnp.sum(dn, axis=0, keepdims=True), norm_at[1]) + collect(dqb, qkv_at)
    dx = (dxh[...] + dn * vec[0:1, :]).astype(BF16)
    dwq = mm_tn(na[...], dqkv[...]).reshape(32, 24, QKV)
    small = small.reshape(32, 8, 128)
    row6 = jnp.concatenate([dwo[:, i : i + 1, 640:] for i in range(5)], axis=2)
    row7 = jnp.concatenate([dwo[:, 5:6, 640:]] + [small[:, i : i + 1] for i in range(4)], axis=2)
    wq[...] = jnp.concatenate([dwq, dwo[:, :6, :640], row6, row7], axis=1).astype(BF16).reshape(4, 4, 2, 32, QKV)

    def qslot(k1, k2, cc):
        return (y + k1 * (1 - cc) + k2 * cc) % 4, (x + k1 * cc + k2 * (1 - cc)) % 4

    order = [(k1, k2) for k1 in (2, 1, 3, 0) for k2 in (2, 1, 3, 0)]
    qsends = []
    for k1, k2 in order:
        yy, xx = qslot(k1, k2, 1 - c)
        d = rcopy(wq.at[yy, xx, 1 - c], qb1.at[k1, k2], qa_s.at[k1, k2], qa_r.at[k1, k2], partner)
        d.start()
        qsends.append(d)
    dxp[...] = mm_nt(dx, s[...]).astype(BF16).reshape(4, 128, 768)
    toks = [rcopy(dxp.at[(z + k) % 4], rd.at[z], t_s.at[k], t_r.at[k], home[k]) for k in range(4)]
    stay = pltpu.make_async_copy(dxp.at[z], rd.at[z], loc.at[1])
    for k in range(1, 4):
        toks[k].start()

    @pl.when(swapped)
    def _():
        toks[0].start()

    @pl.when(xhi == c)
    def _():
        stay.start()

    for k1, k2 in order:
        yy, xx = qslot(k1, k2, c)
        rcopy(wq.at[yy, xx, c], qb1.at[k1, k2], qa_s.at[k1, k2], qa_r.at[k1, k2], partner).wait_recv()
        qpair[k1, k2] = (wq[yy, xx, c].astype(F32) + qb1[k1, k2].astype(F32)).astype(BF16)
        if k1:
            d = rcopy(qpair.at[k1, k2], qb2.at[4 - k1, k2], qb_s.at[k1, k2], qb_r.at[4 - k1, k2], second[k1])
            d.start()
            qsends.append(d)
    for k2 in (2, 1, 3, 0):
        for k1 in range(1, 4):
            rcopy(qpair.at[k1, k2], qb2.at[k1, k2], qb_s.at[k1, k2], qb_r.at[k1, k2], partner).wait_recv()
        total = qpair[0, k2].astype(F32) + qb2[1, k2].astype(F32) + qb2[2, k2].astype(F32) + qb2[3, k2].astype(F32)
        if k2:
            qquad[k2] = total.astype(BF16)
            d = rcopy(qquad.at[k2], qb3.at[4 - k2], qc_s.at[k2], qc_r.at[4 - k2], first[k2])
            d.start()
            qsends.append(d)
    for k in range(1, 4):
        rcopy(qquad.at[k], qb3.at[k], qc_s.at[k], qc_r.at[k], partner).wait_recv()
    m_last()
    total = total + qb3[1].astype(F32) + qb3[2].astype(F32) + qb3[3].astype(F32)
    for i in range(4):
        zs[i, 0:6, :QKV] = total[6 * i : 6 * i + 6]
        zs[i, 0:6, QKV : QKV + UP] = fm[6 * i : 6 * i + 6, :]
        zs[i, 0:1, QKV + UP :] = total[31:32, 128 + 128 * i : 256 + 128 * i]
    zsends = [rcopy(zs.at[(z + k) % 4], zr.at[z], ze_s.at[k], ze_r.at[4 - k], zpeer[k]) for k in range(1, 4)]
    for d in zsends:
        d.start()
    zr[z] = zs[z]
    dn_out[...] = fm[24:, :]
    o8_out[...] = total[24:32]

    for d in qsends + msends + ysends + halves + kvsends + [msend]:
        d.wait_send()
    for k in range(1, 4):
        toks[k].wait()

    @pl.when(swapped)
    def _():
        out_swap.wait()
        toks[0].wait()

    @pl.when(xhi == c)
    def _():
        out_stay.wait()
        stay.wait()

    for d in zsends:
        d.wait()


def layer(*args):
    sh = jax.ShapeDtypeStruct

    def vm(*shape, dtype=BF16):
        return pltpu.VMEM(shape, dtype)

    def sem(*shape):
        return pltpu.SemaphoreType.DMA(shape)

    tok = (4, 128, 768)
    scratch = [
        vm(*tok), vm(*tok), vm(4, 4, 2, 32, QKV), vm(4, 4, 2, 48, 768), vm(4, 8, ZW, dtype=F32), vm(4, 8, ZW, dtype=F32),
        vm(32, QKV), vm(48, 768), vm(768, 768), vm(3, 128, 256), vm(512, 4096, dtype=F32), vm(512, 768, dtype=F32),
        vm(512, 768), vm(512, 768), vm(8, 768, dtype=F32), vm(3, 4, 8, 128, 128), vm(3, 1024, 128),
        vm(3, 4, 4, 2, 128, 128), vm(512, 768), vm(512, 768), vm(512, 768, dtype=F32), vm(512, 768, dtype=F32),
        vm(256, 768), vm(768, 768), vm(768, QKV), vm(512, 256), vm(512, QKV), vm(*tok), vm(*tok), vm(*tok), vm(48, 768, dtype=F32),
    ] + [vm(512, 128, dtype=F32)] * 7 + [
        vm(3, 4, 4, 128, 128), vm(3, 4, 4, 128, 128), vm(3, 4, 4, 128, 128),
        vm(4, 4, 48, 768), vm(4, 4, 48, 768), vm(4, 4, 48, 768), vm(4, 48, 768), vm(4, 48, 768),
        vm(4, 4, 32, QKV), vm(4, 4, 32, QKV), vm(4, 4, 32, QKV), vm(4, 32, QKV), vm(4, 32, QKV),
        sem(2), sem(2), sem(2), sem(2, 4), sem(2, 4), sem(4), sem(4),
        sem(4), sem(4, 4), sem(4, 4), sem(4, 4), sem(4, 4), sem(4), sem(4, 4), sem(4, 4), sem(4, 4), sem(4, 4),
        sem(3, 4), sem(3, 4), sem(3, 4), sem(3, 4), sem(3), sem(3), sem(3, 4), sem(3, 4),
        sem(1), sem(1), sem(4), sem(4), sem(4), sem(4), sem(4, 4), sem(4, 4), sem(4, 4), sem(4, 4), sem(4), sem(4),
        sem(4), sem(4), sem(4), sem(4), sem(4), sem(4),
    ]
    return pl.pallas_call(
        layer_kernel,
        out_shape=(sh((128, 768), BF16), sh(tok, BF16), sh((4, 8, ZW), F32), sh((24, 768), F32), sh((8, 640), F32)),
        in_specs=[VMEM] * 14,
        out_specs=(HBM, HBM, VMEM, VMEM, VMEM),
        scratch_shapes=scratch,
        compiler_params=pltpu.CompilerParams(vmem_limit_bytes=63 * MIB, collective_id=0, has_side_effects=True),
        name="layer",
    )(*args)


CUTS = (0, 18, 24, 48, 54, 60, 66, 72, 78)


def finish_kernel(x_ref, g_ref, ro, rd, zr, dn, o8, *outs):
    out, dx_out, qkv, up, out_w, down = outs[:6]
    xf = x_ref[...].astype(F32)
    out[0] = ro[...]
    dxh = rd[0].astype(F32) + rd[1].astype(F32) + rd[2].astype(F32) + rd[3].astype(F32)
    cen = xf - jnp.mean(xf, axis=1, keepdims=True)
    rstd = lax.rsqrt(jnp.mean(cen * cen, axis=1, keepdims=True) + 1e-5)
    xn = cen * rstd
    mean, along = jnp.mean(dxh, axis=1, keepdims=True), jnp.mean(dxh * xn, axis=1, keepdims=True)
    dx_out[0] = g_ref[...].astype(F32) + rstd * (dxh - mean - xn * along)
    pieces = [zr[i, 0:6, 384:576] for i in range(4)]
    pieces += [zr[i, 0:6, 128 * h : 128 * h + 64] for i in range(4) for h in range(3)]
    pieces += [zr[i, 0:6, 128 * h + 64 : 128 * h + 128] for i in range(4) for h in range(3)]
    qkv[:, 0, :] = jnp.concatenate(pieces, axis=1)
    up[:, 0, :] = jnp.concatenate([zr[i, 0:6, QKV : QKV + UP] for i in range(4)], axis=1)
    tails = [o8[6:7, 128 * i : 128 * i + 128] for i in range(5)] + [o8[7:8, :128]]
    out_w[:, 0, :] = jnp.concatenate([o8[0:6, :], jnp.concatenate(tails, axis=0)], axis=1)
    down[0] = dn[...]
    rows = sum(zr[i, 0:1, QKV + UP :] for i in range(4))
    for ref, a, b in zip(outs[6:], CUTS[:-1], CUTS[1:]):
        ref[...] = rows[:, a:b]


def finish(*args):
    def sh(*shape, dtype=F32):
        return jax.ShapeDtypeStruct(shape, dtype)

    shapes = [sh(1, 128, 768, dtype=BF16), sh(1, 128, 768), sh(6, 1, 2304), sh(6, 1, 3072), sh(6, 1, 768), sh(1, 24, 768)]
    shapes += [sh(1, b - a) for a, b in zip(CUTS[:-1], CUTS[1:])]
    return pl.pallas_call(
        finish_kernel,
        out_shape=tuple(shapes),
        in_specs=[VMEM] * 7,
        out_specs=(VMEM,) * 14,
        compiler_params=params(),
        name="finish",
    )(*args)


def body(
    inputs, qkv_weight, qkv_bias, out_weight, out_bias, up_weight, up_bias, down_weight, down_bias,
    attn_gain, attn_shift, mlp_gain, mlp_shift, cotangent,
):
    x, g = inputs[0], cotangent[0]
    vectors = (qkv_bias, out_bias, up_bias, down_bias, attn_gain, attn_shift, mlp_gain, mlp_shift)
    ro, rd, zr, dn, o8 = layer(x, g, qkv_weight, up_weight, out_weight, down_weight, *vectors)
    out, dx, qkv, up, ow, dw, *t = finish(x, g, ro, rd, zr, dn, o8)
    qkv, up, ow = qkv.transpose(1, 0, 2), up.transpose(1, 0, 2), ow.transpose(1, 0, 2)
    return out, dx, qkv, t[0], ow, t[1], up, t[2], dw, t[3], t[4], t[5], t[6], t[7]


def solution(mesh):
    tok = P("fsdp", "ctx", None)
    mat = P(None, ("ctx", "fsdp"), None)
    row = P(None, ("ctx", "fsdp"))
    in_specs = (tok, mat, row, mat, row, mat, row, mat, row, row, row, row, row, tok)
    out_specs = (tok, tok, mat, row, mat, row, mat, row, mat, row, row, row, row, row)
    return jax.shard_map(body, mesh=mesh, in_specs=in_specs, out_specs=out_specs, check_vma=False)
```

```python
import functools

import jax
import jax.numpy as jnp
import numpy as np
from jax import lax
from jax.experimental import pallas as pl
from jax.experimental.pallas import tpu as pltpu
from jax.sharding import PartitionSpec as P

F32 = jnp.float32
BF16 = jnp.bfloat16
MESH = pl.DeviceIdType.MESH
VMEM = pl.BlockSpec(memory_space=pltpu.VMEM)
HBM = pl.BlockSpec(memory_space=pl.ANY)
MIB = 1024 * 1024

QKV, UP = 640, 768
EARLY = 512
KV_AT, Q_AT = (0, 128, 512), 256
ZW = QKV + UP + 128
OFF = -1e30

def place():
    ctx, fs = lax.axis_index("ctx"), lax.axis_index("fsdp")
    z, y, xh = ctx // 8, (ctx // 2) % 4, ctx % 2
    xl, c = fs // 2, fs % 2
    return z, y, xh, xl, c


def dev(z, y, x, c):
    return (z * 8 + y * 2 + x // 2, (x % 2) * 2 + c)


def rcopy(src, dst, ss, rs, to):
    return pltpu.make_async_remote_copy(
        src_ref=src, dst_ref=dst, send_sem=ss, recv_sem=rs, device_id=to, device_id_type=MESH
    )


def mm(a, b):
    return jnp.dot(a, b, preferred_element_type=F32)


def mm_nt(a, b):
    return lax.dot_general(a, b, (((1,), (1,)), ((), ())), preferred_element_type=F32)


def mm_tn(a, b):
    return lax.dot_general(a, b, (((0,), (0,)), ((), ())), preferred_element_type=F32)


def params(**kw):
    return pltpu.CompilerParams(vmem_limit_bytes=60 * MIB, **kw)


def ids(shape, axis):
    return lax.broadcasted_iota(jnp.int32, shape, axis)


def div(n, d):
    return ((n.astype(F32) + 0.5) * np.float32(1.0 / d)).astype(jnp.int32)


def one_hot(mask):
    return jnp.where(mask, 1.0, 0.0).astype(BF16)


def owner(j):
    p = div(j, 24)
    return p, j - 24 * p


def vector_places(z):
    j = ids((1, 768), 1)
    p, of = owner(j)
    norms = [(8 * p + div(of, 6), [at + of - 6 * div(of, 6)]) for at in (54, 60, 66, 72)]
    m = ids((1, QKV), 1)
    is_q = (m >= Q_AT) & (m < EARLY)
    kind = jnp.where(is_q, 0, jnp.where(m % 128 < 64, 1, 2))
    head = jnp.where(m < EARLY, m // 128, 2)
    col = kind * 768 + 192 * z + jnp.where(is_q, m - Q_AT, 64 * head + m % 64)
    own = div(col, 18)
    qkv = ((own % 32) * 8 + own // 32, [jnp.where(is_q & (m >= Q_AT + 192), -1, col - 18 * own)])
    f = ids((1, UP), 1)
    p = div(f, 24)
    up = (p * 8 + z, [24 + f - 24 * p])
    own = div(f, 6)
    r = f - 6 * own
    out = ((own % 32) * 8 + own // 32, [18 + r, 48 + r])
    return norms, qkv, up, out


def lane_hot(lanes, n):
    lane = ids((128, n), 0)
    hit = lane == lanes[0]
    for more in lanes[1:]:
        hit = hit | (lane == more)
    return one_hot(hit)


def spread(packed, where):
    row, lanes = where
    n = row.shape[1]
    t = mm(packed, lane_hot(lanes, n))
    return jnp.sum(jnp.where(ids((256, n), 0) == row, t, 0.0), axis=0, keepdims=True)


def collect(vector, where):
    row, lanes = where
    n = row.shape[1]
    t = jnp.where(ids((256, n), 0) == row, vector, 0.0).astype(BF16)
    return mm_nt(t, lane_hot(lanes, n))


def turn(tile, cos, plus, minus):
    return tile * cos + pltpu.roll(tile, 8, 1) * plus + pltpu.roll(tile, 120, 1) * minus


def layer_kernel(
    x_ref, g_ref, qw_ref, uw_ref, ow_ref, dw_ref, v0, v1, v2, v3, v4, v5, v6, v7,
    ro, rd, zr, dn_out, o8_out,
    xa, ga, wq, wm, zs, zb, cq, cm, s, s3, big, xh, na, nm, vec, kv, qd, dkv, hid, du, part, dxh,
    ow, dw, wn, att, dqkv, outp, obuf, dxp, cos_ref, sp_ref, sm_ref, top, tot, acc, delta,
    kb1, kpair, kb2, mb1, mpair, mb2, mquad, mb3, eb1, epair, eb2, equad, eb3, lb1, lpair, lb2, lquad, lb3,
    swap_s, swap_r, loc, tz_s, tz_r, wz_s, wz_r,
    q1_s, q2_s, q3_s, qr_r, qp_r, m1_s, m2_s, m3_s, mr_r, mp_r,
    ky_s, ky_r, kh_s, kh_r, kp_s, kp_r, dp_s, dp_r, dy_s, dy_r,
    ma_s, ma_r, mb_s, mb_r, mc_s, mc_r, ea_s, ea_r, eb_s, eb_r, ec_s, ec_r, la_s, la_r, lb_s, lb_r, lc_s, lc_r,
    t_s, t_r, o_s, o_r, ze_s, ze_r,
):
    z, y, xhi, xl, c = place()
    x = xhi * 2 + xl
    zpeer = [dev((z + k) % 4, y, x, c) for k in range(4)]
    ypeer = [dev(z, (y + k) % 4, x, c) for k in range(4)]
    xpeer = [dev(z, y, (x + k) % 4, c) for k in range(4)]
    home = [dev((z + k) % 4, y, c * 2 + xl, xhi) for k in range(4)]
    first = [dev(z, (y + k * c) % 4, (x + k * (1 - c)) % 4, c) for k in range(4)]
    second = [dev(z, (y + k * (1 - c)) % 4, (x + k * c) % 4, c) for k in range(4)]
    partner = dev(z, y, x, 1 - c)
    swapped = xhi != c

    def q_slot(k1, k2, cc):
        return (y + k1 * cc + k2 * (1 - cc)) % 4, (x + k1 * (1 - cc) + k2 * cc) % 4

    bar = pltpu.get_barrier_semaphore()
    for to in zpeer[1:] + ypeer[1:] + xpeer[1:] + [partner]:
        pl.semaphore_signal(bar, inc=1, device_id=to, device_id_type=MESH)

    @pl.when(swapped)
    def _():
        for to in home:
            pl.semaphore_signal(bar, inc=1, device_id=to, device_id_type=MESH)

    zs[...] = jnp.zeros((4, 8, ZW), F32)
    qw = qw_ref[0].astype(F32)
    uw = uw_ref[0].astype(F32)
    vectors = [v[...].astype(F32) for v in (v0, v1, v2, v3, v4, v5, v6, v7)]
    vectors = jnp.concatenate(vectors + [jnp.zeros((1, 50), F32)], axis=1)
    for i in range(4):
        pieces = []
        for h in range(3):
            at = 192 * i + 64 * h
            pieces += [qw[:, 768 + at : 832 + at], qw[:, 1536 + at : 1600 + at]]
        pieces[4:4] = [qw[:, 192 * i : 192 * i + 192], jnp.zeros((6, 64), F32)]
        zs[i, 0:6, :QKV] = jnp.concatenate(pieces, axis=1)
        zs[i, 0:6, QKV : QKV + UP] = uw[:, UP * i : UP * i + UP]
        zs[i, 0:1, QKV + UP :] = vectors

    pl.semaphore_wait(bar, 10 + 4 * ((xhi + c) % 2))

    zsends = [rcopy(zs.at[(z + k) % 4], zb.at[z], wz_s.at[k], wz_r.at[4 - k], zpeer[k]) for k in range(1, 4)]
    for d in zsends:
        d.start()
    swaps = [rcopy(src, dst.at[z], swap_s.at[t], swap_r.at[t], home[0]) for t, (src, dst) in enumerate(((x_ref, xa), (g_ref, ga)))]

    @pl.when(swapped)
    def _():
        swaps[0].start()
        swaps[1].start()

    @pl.when(xhi == c)
    def _():
        xa[z] = x_ref[...]
        ga[z] = g_ref[...]

    zb[z] = zs[z]
    p, of = owner(ids((1, 768), 1))
    nat = 192 * div(of, 6) + 6 * p + of - 6 * div(of, 6)
    s[...] = one_hot(ids((768, 768), 0) == nat)
    i8 = ids((1, 256), 1)
    nat8 = jnp.where(i8 % 8 < 6, 6 * (i8 // 8) + i8 % 8, -1)
    for h in range(3):
        dim = ids((128, 256), 0)
        s3[h] = one_hot((dim >= 64) & (dim + (64 * h - 64) == nat8))

    for d in zsends:
        d.wait()
    rows = [zb[i, 0:6, :] for i in range(4)]
    rows = jnp.concatenate(rows, axis=0)
    out8 = ow_ref[0].astype(F32)
    tails = [out8[i : i + 1, 640:] for i in range(6)]
    row6 = jnp.concatenate(tails[:5], axis=1)
    row7 = jnp.concatenate(tails[5:] + [zb[i, 0:1, QKV + UP :] for i in range(4)], axis=1)
    cq[...] = jnp.concatenate([rows[:, :QKV], out8[:, :640], row6, row7], axis=0).astype(BF16)
    cm[...] = jnp.concatenate([rows[:, QKV : QKV + UP], dw_ref[0].astype(F32)], axis=0).astype(BF16)
    wq[y, x, c] = cq[...]
    wm[y, x, c] = cm[...]

    class Ring:
        def __init__(self, own, arr, slot, one, two, s1, s2, s3s, rr, pr):
            self.slot, self.one, self.two = slot, one, two
            self.own, self.arr, self.s1, self.s2, self.s3, self.rr, self.pr, self.sends = own, arr, s1, s2, s3s, rr, pr, []

        def send(self, src, yy, xx, ss, rs, to):
            d = rcopy(src, self.arr.at[yy, xx, c], ss, rs, to)
            d.start()
            self.sends.append(d)

        def begin(self):
            for k in range(1, 4):
                self.send(self.own, y, x, self.s1.at[k], self.rr.at[4 - k, 0], self.one[k])
            for k in range(1, 4):
                self.send(self.own, y, x, self.s2.at[0, k], self.rr.at[0, 4 - k], self.two[k])
            self.send(self.own, y, x, self.s3.at[0, 0], self.pr.at[0, 0], partner)

        def arrived(self, k1, k2, rs, cc):
            yy, xx = self.slot(k1, k2, cc)
            ref = self.arr.at[yy, xx, cc]
            rcopy(ref, ref, self.s3.at[k1, k2], rs, partner).wait_recv()
            return yy, xx

        def forward(self, k1, k2, on):
            yy, xx = self.arrived(k1, k2, self.rr.at[k1, k2], c)
            src = self.arr.at[yy, xx, c]
            if on:
                for k in range(1, 4):
                    self.send(src, yy, xx, self.s2.at[k1, k], self.rr.at[k1, 4 - k], self.two[k])
            self.send(src, yy, xx, self.s3.at[k1, k2], self.pr.at[k1, k2], partner)

        def finish(self):
            for k1 in range(4):
                for k2 in range(4):
                    yy, xx = self.slot(k1, k2, 1 - c)
                    ref = self.arr.at[yy, xx, 1 - c]
                    rcopy(ref, ref, self.s3.at[k1, k2], self.pr.at[k1, k2], partner).wait_recv()
            for d in self.sends:
                d.wait_send()

    rq = Ring(cq, wq, q_slot, first, second, q1_s, q2_s, q3_s, qr_r, qp_r)
    rm = Ring(cm, wm, q_slot, first, second, m1_s, m2_s, m3_s, mr_r, mp_r)
    rq.begin()

    def spread_tokens(t, arr):
        @pl.when(swapped)
        def _():
            swaps[t].wait()

        ds = [rcopy(arr.at[z], arr.at[z], tz_s.at[t, k], tz_r.at[t, 4 - k], zpeer[k]) for k in range(1, 4)]
        for d in ds:
            d.start()
        return ds

    xtok = spread_tokens(0, xa)
    rm.begin()
    for k1 in range(1, 4):
        rq.forward(k1, 0, True)
    gtok = spread_tokens(1, ga)
    for k1 in range(1, 4):
        rm.forward(k1, 0, True)

    lane = ids((128, 128), 1) % 64
    freq = jnp.exp((lane % 8).astype(F32) * np.float32(-2.0 / 16 * np.log(10000.0)))
    freq = jnp.where(lane < 16, freq, 0.0)
    yc = 2 * y + c
    for i in range(4):
        r = slice(128 * i, 128 * i + 128)
        angle = ((8 * i + yc) * 128 + ids((128, 128), 0)).astype(F32) * freq
        sin = jnp.sin(angle)
        cos_ref[r, :] = jnp.cos(angle)
        sp_ref[r, :] = jnp.where(lane >= 8, sin, 0.0)
        sm_ref[r, :] = jnp.where(lane < 8, -sin, 0.0)
    for d in xtok:
        d.wait()
    big[:, :768] = mm(xa[...].reshape(512, 768), s[...])
    for k2 in range(1, 4):
        for k1 in range(4):
            rq.forward(k1, k2, False)
    for i in range(4):
        r = slice(128 * i, 128 * i + 128)
        v = big[r, :768]
        cen = v - jnp.sum(v, axis=1, keepdims=True) * (1.0 / 768.0)
        var = jnp.sum(cen * cen, axis=1, keepdims=True) * (1.0 / 768.0)
        xh[r, :] = cen * lax.rsqrt(var + 1e-5)
    rq.finish()
    rest = wq[...].reshape(32, 32, QKV).astype(F32)
    wqkv = rest[:, :24].reshape(768, QKV).astype(BF16)
    rest = rest[:, 24:]
    packed = [rest[:, 7:8, 128 + 128 * i : 256 + 128 * i] for i in range(4)] + [jnp.zeros((32, 4, 128), F32)]
    packed = jnp.concatenate(packed, axis=1).reshape(256, 128).astype(BF16)
    norm_at, qkv_at, up_at, out_at = vector_places(z)
    for i in range(4):
        vec[i : i + 1, :] = spread(packed, norm_at[i])
    for i in range(4):
        r = slice(128 * i, 128 * i + 128)
        na[r, :] = (xh[r, :] * vec[0:1, :] + vec[1:2, :]).astype(BF16)
        nm[r, :] = (xh[r, :] * vec[2:3, :] + vec[3:4, :]).astype(BF16)

    wn[...] = wqkv
    big[:, 1024 : 1024 + QKV] = mm(na[...], wqkv) + spread(packed, qkv_at)
    low = ids((128, 128), 1) < 64
    for i in range(4):
        r = slice(128 * i, 128 * i + 128)
        cos, plus, minus = cos_ref[r, :], sp_ref[r, :], sm_ref[r, :]
        kc, kp, km = jnp.where(low, cos, 1.0), jnp.where(low, plus, 0.0), jnp.where(low, minus, 0.0)
        for h in range(3):
            kv[h, i, yc] = turn(big[r, 1024 + KV_AT[h] : 1152 + KV_AT[h]], kc, kp, km).astype(BF16)
        q01 = turn(big[r, 1024 + Q_AT : 1152 + Q_AT], cos, plus, minus).astype(BF16).astype(F32) * 0.125
        q2 = turn(big[r, 1152 + Q_AT : 1280 + Q_AT], cos, plus, minus).astype(BF16).astype(F32) * 0.125
        qd[0, r, :] = jnp.where(low, q01, 0.0).astype(BF16)
        qd[1, r, :] = jnp.where(low, pltpu.roll(q01, 64, 1), 0.0).astype(BF16)
        qd[2, r, :] = jnp.where(low, q2, 0.0).astype(BF16)

    kvsends = []

    def kv_send(src, ss, rs, to):
        d = rcopy(src, src, ss, rs, to)
        d.start()
        kvsends.append(d)

    for h in range(3):
        mine = kv.at[h, :, yc]
        kv_send(mine, ky_s.at[h, 1], ky_r.at[h, 3], ypeer[1])
        kv_send(mine, ky_s.at[h, 3], ky_r.at[h, 1], ypeer[3])
        kv_send(mine, kp_s.at[h, 0], kp_r.at[h, 0], partner)

    def pass_on(h):
        for k in (1, 3):
            at = 2 * ((y + k) % 4) + c
            there = kv.at[h, :, at]
            rcopy(there, there, ky_s.at[h, k], ky_r.at[h, k], partner).wait_recv()
            part_of = kv.at[h, 0:2, at] if k == 3 else kv.at[h, 2:4, at]
            kv_send(part_of, kh_s.at[h, k], kh_r.at[h, k], ypeer[4 - k])
            kv_send(there, kp_s.at[h, k], kp_r.at[h, k], partner)

    def pass_far(h):
        at = 2 * ((y + 2) % 4) + c
        for k in (1, 3):
            part_of = kv.at[h, 0:2, at] if k == 3 else kv.at[h, 2:4, at]
            rcopy(part_of, part_of, kh_s.at[h, k], kh_r.at[h, k], partner).wait_recv()
        kv_send(kv.at[h, :, at], kp_s.at[h, 2], kp_r.at[h, 2], partner)

    def kv_here(h):
        for k in range(4):
            there = kv.at[h, :, 2 * ((y + k) % 4) + 1 - c]
            rcopy(there, there, kp_s.at[h, k], kp_r.at[h, k], partner).wait_recv()

    for d in gtok:
        d.wait()
    tails = [rest[:, 6:7, 128 * i : 128 * i + 128] for i in range(5)] + [rest[:, 7:8, :128], jnp.zeros((32, 2, 128), F32)]
    ow[:, :640] = rest.reshape(256, 640).astype(BF16)
    ow[:, 640:] = jnp.concatenate(tails, axis=1).reshape(256, 128).astype(BF16)
    g = ga[...].reshape(512, 768)
    dof = mm_nt(g, ow[...]).astype(BF16)
    for h in range(3):
        qd[h, 512:, :] = mm_nt(dof, s3[h]).astype(BF16)
    for k2 in range(1, 4):
        for k1 in range(4):
            rm.forward(k1, k2, False)
    pass_on(0)
    rm.finish()
    pass_on(1)

    class Sum:
        def __init__(self, arr, lanes, y_first, b1, pair, b2, quad, b3, sems):
            self.arr, self.lanes, self.b1, self.pair, self.b2, self.quad, self.b3 = arr, lanes, b1, pair, b2, quad, b3
            self.as_, self.ar, self.bs, self.br, self.cs, self.cr = sems
            self.sends, self.y_first = [], y_first
            self.one_peer, self.two_peer = (ypeer, xpeer) if y_first else (xpeer, ypeer)

        def begin(self):
            src = self.arr.at[:, :, 1 - c, :, self.lanes]
            self.sends.append(rcopy(src, self.b1, self.as_.at[0], self.ar.at[0], partner))
            self.sends[0].start()

        def one(self, k1, k2):
            yy, xx = ((y + k1) % 4, (x + k2) % 4) if self.y_first else ((y + k2) % 4, (x + k1) % 4)
            return (self.arr[yy, xx, c, :, self.lanes].astype(F32) + self.b1[yy, xx].astype(F32)).astype(BF16)

        def pairs(self):
            self.sends[0].wait_recv()
            for k in (2, 1, 3):
                for k2 in range(4):
                    self.pair[k, k2] = self.one(k, k2)
                d = rcopy(self.pair.at[k], self.b2.at[4 - k], self.bs.at[k], self.br.at[4 - k], self.one_peer[k])
                d.start()
                self.sends.append(d)
            for k2 in range(4):
                self.pair[0, k2] = self.one(0, k2)

        def quads(self):
            for k in range(1, 4):
                rcopy(self.pair.at[k], self.b2.at[k], self.bs.at[k], self.br.at[k], partner).wait_recv()
            for k in (2, 1, 3, 0):
                total = self.pair[0, k].astype(F32)
                for i in range(1, 4):
                    total += self.b2[i, k].astype(F32)
                if k:
                    self.quad[k] = total.astype(BF16)
                    d = rcopy(self.quad.at[k], self.b3.at[4 - k], self.cs.at[k], self.cr.at[4 - k], self.two_peer[k])
                    d.start()
                    self.sends.append(d)
            self.mine = total

        def last(self):
            total = self.mine
            for k in range(1, 4):
                rcopy(self.quad.at[k], self.b3.at[k], self.cs.at[k], self.cr.at[k], partner).wait_recv()
                total += self.b3[k].astype(F32)
            return total

        def drain(self):
            for d in self.sends:
                d.wait_send()

    sum_m = Sum(wm, slice(0, 768), False, mb1, mpair, mb2, mquad, mb3, (ma_s, ma_r, mb_s, mb_r, mc_s, mc_r))
    sum_e = Sum(wq, slice(0, EARLY), True, eb1, epair, eb2, equad, eb3, (ea_s, ea_r, eb_s, eb_r, ec_s, ec_r))
    sum_l = Sum(wq, slice(EARLY, QKV), True, lb1, lpair, lb2, lquad, lb3, (la_s, la_r, lb_s, lb_r, lc_s, lc_r))

    w48 = wm[...].reshape(32, 48, 768).astype(F32)
    dw[...] = w48[:, 24:].reshape(768, 768).astype(BF16)
    wup = w48[:, :24].reshape(768, UP).astype(BF16)
    lanes = slice(2048, 2048 + UP)
    big[:, lanes] = mm(nm[...], wup) + spread(packed, up_at)
    pass_far(0)
    pass_on(2)
    for i in range(4):
        r = slice(128 * i, 128 * i + 128)
        u = big[r, lanes]
        cdf = 0.5 * (1.0 + lax.erf(u * np.float32(np.sqrt(0.5))))
        pdf = jnp.exp(-0.5 * u * u) * np.float32(1.0 / np.sqrt(2.0 * np.pi))
        hid[r, :] = (u * cdf).astype(BF16)
        big[r, lanes] = cdf + u * pdf
    part[...] = mm(hid[...], dw[...])
    du[...] = (mm_nt(g, dw[...]) * big[:, lanes]).astype(BF16)
    pass_far(1)
    dn = mm_nt(du[...], wup)
    grads = [
        jnp.sum(dn * xh[...], axis=0, keepdims=True),
        jnp.sum(dn, axis=0, keepdims=True),
        jnp.sum(du[...].astype(F32), axis=0, keepdims=True),
    ]
    dxh[...] = dn * vec[2:3, :]
    small = collect(grads[0], norm_at[2]) + collect(grads[1], norm_at[3]) + collect(grads[2], up_at)
    small += collect(jnp.sum(ga[z].astype(F32), axis=0, keepdims=True), out_at)
    dwu = mm_tn(nm[...], du[...]).reshape(32, 24, 768)
    dwd = mm_tn(hid[...], g).reshape(32, 24, 768)
    wm[...] = jnp.concatenate([dwu, dwd], axis=1).astype(BF16).reshape(4, 4, 2, 48, 768)
    sum_m.begin()
    pass_far(2)

    row = yc * 128 + ids((128, 1024), 0)
    key = ids((128, 1024), 1)

    def rep(a):
        return jnp.concatenate([a] * 8, axis=1)

    def fold(a, f):
        r = a[:, :128]
        for i in range(1, 8):
            r = f(r, a[:, 128 * i : 128 * i + 128])
        return r

    def keys_of(h, j):
        return kv[h, j].reshape(1024, 128)

    def lane_sum(a, f):
        return jnp.broadcast_to(f(a, axis=1, keepdims=True), (512, 128))

    def attend(h, middle):
        top[...] = jnp.full((512, 128), OFF, F32)
        tot[...] = jnp.zeros((512, 128), F32)
        acc[...] = jnp.zeros((512, 128), F32)
        for j in range(4):
            r0, cols = 128 * j, slice(1024 * j, 1024 * j + 1024)
            sc = mm_nt(qd[h, r0:512, :], keys_of(h, j))
            near = jnp.where(key <= row, sc[:128], OFF)
            sc = near if j == 3 else jnp.concatenate([near, sc[128:]], axis=0)
            big[r0:, cols] = sc
            top[r0:, :] = jnp.maximum(top[r0:, :], fold(sc, jnp.maximum))
        top[...] = lane_sum(top[...], jnp.max)
        for j in range(4):
            r0, cols = 128 * j, slice(1024 * j, 1024 * j + 1024)
            p = jnp.exp(big[r0:, cols] - rep(top[r0:, :]))
            big[r0:, cols] = p
            tot[r0:, :] += fold(p, jnp.add)
            acc[r0:, :] += mm(p.astype(BF16), keys_of(h, j))
        inv = 1.0 / lane_sum(tot[...], jnp.sum)
        tot[...] = inv
        o = acc[...] * inv
        delta[...] = lane_sum(o * qd[h, 512:, :].astype(F32), jnp.sum)
        acc[...] = jnp.zeros((512, 128), F32)
        middle()
        for j in range(4):
            r0, cols = 128 * j, slice(1024 * j, 1024 * j + 1024)
            kvj = keys_of(h, j)
            p = big[r0:, cols] * rep(tot[r0:, :])
            dp = mm_nt(qd[h, 512 + r0 :, :], kvj)
            ds = (p * (dp - rep(delta[r0:, :]))).astype(BF16)
            acc[r0:, :] += mm(ds, kvj)
            d = mm_tn(qd[h, r0:512, :], ds) + mm_tn(qd[h, 512 + r0 :, :], p.astype(BF16))
            for i in range(8):
                dkv[h, j, i // 2, i % 2] = d[:, 128 * i : 128 * i + 128].astype(BF16)
        return mm(o.astype(BF16), s3[h]), acc[...] * 0.125

    halves, ysends = [], []

    def dkv_begin(h):
        d = rcopy(dkv.at[h, :, :, 1 - c], kb1.at[h], dp_s.at[h], dp_r.at[h], partner)
        d.start()
        halves.append(d)

    def dkv_pairs(h):
        halves[h].wait_recv()
        for k in (2, 1, 3, 0):
            yy = (y + k) % 4
            for i in range(4):
                kpair[h, k, i] = (dkv[h, i, yy, c].astype(F32) + kb1[h, i, yy].astype(F32)).astype(BF16)
            if k:
                d = rcopy(kpair.at[h, k], kb2.at[h, 4 - k], dy_s.at[h, k], dy_r.at[h, 4 - k], ypeer[k])
                d.start()
                ysends.append(d)

    def back_tile(i, first_lane, tile, keys):
        r = slice(128 * i, 128 * i + 128)
        cos, plus, minus = cos_ref[r, :], -sp_ref[r, :], -sm_ref[r, :]
        if keys:
            cos, plus, minus = jnp.where(low, cos, 1.0), jnp.where(low, plus, 0.0), jnp.where(low, minus, 0.0)
        dqkv[r, first_lane : first_lane + 128] = turn(tile, cos, plus, minus).astype(BF16)

    def dkv_last(h):
        for k in range(1, 4):
            rcopy(kpair.at[h, k], kb2.at[h, k], dy_s.at[h, k], dy_r.at[h, k], partner).wait_recv()
        for i in range(4):
            total = kpair[h, 0, i].astype(F32) + kb2[h, 1, i].astype(F32) + kb2[h, 2, i].astype(F32) + kb2[h, 3, i].astype(F32)
            back_tile(i, KV_AT[h], total.T, True)

    kv_here(0)
    o0, d0 = attend(0, lambda: None)
    dkv_begin(0)
    sum_m.pairs()
    kv_here(1)
    o1, d1 = attend(1, lambda: dkv_pairs(0))
    dkv_begin(1)
    kv_here(2)
    o2, d2 = attend(2, lambda: dkv_pairs(1))
    dkv_begin(2)

    att[...] = (o0 + o1 + o2).astype(BF16)
    outs = part[...] + mm(att[...], ow[...]) + spread(packed, out_at) * jnp.where(z == 0, 1.0, 0.0)
    outp[...] = outs.astype(BF16).reshape(4, 128, 768)
    osends = [rcopy(outp.at[(z + k) % 4], obuf.at[z], o_s.at[k], o_r.at[4 - k], zpeer[k]) for k in range(1, 4)]
    for d in osends:
        d.start()
    dkv_pairs(2)
    dwo = mm_tn(att[...], g).reshape(32, 8, 768)
    for i in range(4):
        r = slice(128 * i, 128 * i + 128)
        back_tile(i, Q_AT, jnp.where(low, d0[r], pltpu.roll(d1[r], 64, 1)), False)
        back_tile(i, Q_AT + 128, jnp.where(low, d2[r], 0.0), False)
    dkv_last(0)
    dkv_last(1)
    dwq = mm_tn(na[...], dqkv[:, :EARLY]).reshape(32, 24, EARLY)
    tail = [dwo[:, i : i + 1, EARLY:] for i in range(6)]
    early = [dwq, dwo[:, :6, :EARLY], jnp.concatenate(tail[0:2], axis=2), jnp.concatenate(tail[2:4], axis=2)]
    wq[:, :, :, :, :EARLY] = jnp.concatenate(early, axis=1).astype(BF16).reshape(4, 4, 2, 32, EARLY)
    sum_e.begin()
    big[:, :768] = mm_nt(dqkv[:, :EARLY], wn[:, :EARLY])
    sum_e.pairs()
    dkv_last(2)

    toks = [rcopy(dxp.at[(z + k) % 4], rd.at[z], t_s.at[k], t_r.at[k], home[k]) for k in range(4)]
    stay = pltpu.make_async_copy(dxp.at[z], rd.at[z], loc.at[1])
    along, plain = jnp.zeros((1, 768), F32), jnp.zeros((1, 768), F32)
    for k in (2, 1, 3, 0):
        i = (z + k) % 4
        r = pl.ds(pl.multiple_of(128 * i, 128), 128)
        dn = big[r, :768] + mm_nt(dqkv[r, EARLY:], wn[:, EARLY:])
        along += jnp.sum(dn * xh[r, :], axis=0, keepdims=True)
        plain += jnp.sum(dn, axis=0, keepdims=True)
        dx = (dxh[r, :] + dn * vec[0:1, :]).astype(BF16)
        dxp[i] = mm_nt(dx, s[...]).astype(BF16)
        if k:
            toks[k].start()

    @pl.when(swapped)
    def _():
        toks[0].start()

    @pl.when(xhi == c)
    def _():
        stay.start()

    dqb = jnp.sum(dqkv[...].astype(F32), axis=0, keepdims=True)
    small += collect(along, norm_at[0]) + collect(plain, norm_at[1]) + collect(dqb, qkv_at)
    dwl = mm_tn(na[...], dqkv[:, EARLY:]).reshape(32, 24, 128)
    rows = [dwl, small.reshape(32, 8, 128)[:, :4]] + [t[:, :, 128 * i : 128 * i + 128] for t in tail[4:] for i in range(2)]
    wq[:, :, :, :, EARLY:] = jnp.concatenate(rows, axis=1).astype(BF16).reshape(4, 4, 2, 32, 128)
    sum_l.begin()
    sum_m.quads()
    for d in osends:
        d.wait()
    obuf[z] = outp[z]
    outs = obuf[0].astype(F32) + obuf[1].astype(F32) + obuf[2].astype(F32) + obuf[3].astype(F32)
    outp[0] = (xa[z].astype(F32) + outs).astype(BF16)
    out_swap = rcopy(outp.at[0], ro, o_s.at[0], o_r.at[0], home[0])
    out_stay = pltpu.make_async_copy(outp.at[0], ro, loc.at[0])

    @pl.when(swapped)
    def _():
        out_swap.start()

    @pl.when(xhi == c)
    def _():
        out_stay.start()

    sum_e.quads()
    sum_l.pairs()
    fm = sum_m.last()
    sum_l.quads()
    fe = sum_e.last()
    dn_out[...] = fm[24:, :]
    fl = sum_l.last()

    for i in range(4):
        r = slice(6 * i, 6 * i + 6)
        zs[i, 0:6, :EARLY] = fe[r]
        zs[i, 0:6, EARLY:QKV] = fl[r]
        zs[i, 0:6, QKV : QKV + UP] = fm[r]
        zs[i, 0:1, QKV + UP :] = fl[24 + i : 25 + i]
    zsends = [rcopy(zs.at[(z + k) % 4], zr.at[z], ze_s.at[k], ze_r.at[4 - k], zpeer[k]) for k in range(1, 4)]
    for d in zsends:
        d.start()
    zr[z] = zs[z]
    o8_out[:, :EARLY] = fe[24:32]
    o8_out[:, EARLY:] = fl[24:32]

    for d in ysends + halves + kvsends:
        d.wait_send()
    for each in (sum_m, sum_e, sum_l):
        each.drain()
    for k in range(1, 4):
        toks[k].wait()

    @pl.when(swapped)
    def _():
        out_swap.wait()
        toks[0].wait()

    @pl.when(xhi == c)
    def _():
        out_stay.wait()
        stay.wait()

    for d in zsends:
        d.wait()


def layer(*args):
    sh = jax.ShapeDtypeStruct

    def vm(*shape, dtype=BF16):
        return pltpu.VMEM(shape, dtype)

    def sem(*shape):
        return pltpu.SemaphoreType.DMA(shape)

    tok = (4, 128, 768)
    scratch = [
        vm(*tok), vm(*tok), vm(4, 4, 2, 32, QKV), vm(4, 4, 2, 48, 768), vm(4, 8, ZW, dtype=F32), vm(4, 8, ZW, dtype=F32),
        vm(32, QKV), vm(48, 768), vm(768, 768), vm(3, 128, 256), vm(512, 4096, dtype=F32), vm(512, 768, dtype=F32),
        vm(512, 768), vm(512, 768), vm(8, 768, dtype=F32), vm(3, 4, 8, 128, 128), vm(3, 1024, 128),
        vm(3, 4, 4, 2, 128, 128), vm(512, 768), vm(512, 768), vm(512, 768, dtype=F32), vm(512, 768, dtype=F32),
        vm(256, 768), vm(768, 768), vm(768, QKV), vm(512, 256), vm(512, QKV), vm(*tok), vm(*tok), vm(*tok),
    ] + [vm(512, 128, dtype=F32)] * 7 + [
        vm(3, 4, 4, 128, 128), vm(3, 4, 4, 128, 128), vm(3, 4, 4, 128, 128),
        vm(4, 4, 48, 768), vm(4, 4, 48, 768), vm(4, 4, 48, 768), vm(4, 48, 768), vm(4, 48, 768),
        vm(4, 4, 32, EARLY), vm(4, 4, 32, EARLY), vm(4, 4, 32, EARLY), vm(4, 32, EARLY), vm(4, 32, EARLY),
        vm(4, 4, 32, 128), vm(4, 4, 32, 128), vm(4, 4, 32, 128), vm(4, 32, 128), vm(4, 32, 128),
        sem(2), sem(2), sem(2), sem(2, 4), sem(2, 4), sem(4), sem(4),
        sem(4), sem(4, 4), sem(4, 4), sem(4, 4), sem(4, 4), sem(4), sem(4, 4), sem(4, 4), sem(4, 4), sem(4, 4),
        sem(3, 4), sem(3, 4), sem(3, 4), sem(3, 4), sem(3, 4), sem(3, 4), sem(3), sem(3), sem(3, 4), sem(3, 4),
    ] + [sem(1), sem(1), sem(4), sem(4), sem(4), sem(4)] * 3 + [
        sem(4), sem(4), sem(4), sem(4), sem(4), sem(4),
    ]
    return pl.pallas_call(
        layer_kernel,
        out_shape=(sh((128, 768), BF16), sh(tok, BF16), sh((4, 8, ZW), F32), sh((24, 768), F32), sh((8, 640), F32)),
        in_specs=[VMEM] * 14,
        out_specs=(HBM, HBM, VMEM, VMEM, VMEM),
        scratch_shapes=scratch,
        compiler_params=pltpu.CompilerParams(vmem_limit_bytes=63 * MIB, collective_id=0, has_side_effects=True),
        name="layer",
    )(*args)


CUTS = (0, 18, 24, 48, 54, 60, 66, 72, 78)


def finish_kernel(x_ref, g_ref, ro, rd, zr, dn, o8, *outs):
    out, dx_out, qkv, up, out_w, down = outs[:6]
    xf = x_ref[...].astype(F32)
    out[0] = ro[...]
    dxh = rd[0].astype(F32) + rd[1].astype(F32) + rd[2].astype(F32) + rd[3].astype(F32)
    cen = xf - jnp.mean(xf, axis=1, keepdims=True)
    rstd = lax.rsqrt(jnp.mean(cen * cen, axis=1, keepdims=True) + 1e-5)
    xn = cen * rstd
    mean, along = jnp.mean(dxh, axis=1, keepdims=True), jnp.mean(dxh * xn, axis=1, keepdims=True)
    dx_out[0] = g_ref[...].astype(F32) + rstd * (dxh - mean - xn * along)
    pieces = [zr[i, 0:6, Q_AT : Q_AT + 192] for i in range(4)]
    pieces += [zr[i, 0:6, KV_AT[h] : KV_AT[h] + 64] for i in range(4) for h in range(3)]
    pieces += [zr[i, 0:6, KV_AT[h] + 64 : KV_AT[h] + 128] for i in range(4) for h in range(3)]
    qkv[:, 0, :] = jnp.concatenate(pieces, axis=1)
    up[:, 0, :] = jnp.concatenate([zr[i, 0:6, QKV : QKV + UP] for i in range(4)], axis=1)
    tails = [o8[6:7, 0:256], o8[6:7, 256:512], o8[7:8, 0:256], o8[7:8, 256:512]]
    tails += [jnp.concatenate([o8[i : i + 1, 512:], o8[i + 1 : i + 2, 512:]], axis=1) for i in (4, 6)]
    out_w[:, 0, :] = jnp.concatenate([o8[0:6, :512], jnp.concatenate(tails, axis=0)], axis=1)
    down[0] = dn[...]
    rows = sum(zr[i, 0:1, QKV + UP :] for i in range(4))
    for ref, a, b in zip(outs[6:], CUTS[:-1], CUTS[1:]):
        ref[...] = rows[:, a:b]


def finish(*args):
    def sh(*shape, dtype=F32):
        return jax.ShapeDtypeStruct(shape, dtype)

    shapes = [sh(1, 128, 768, dtype=BF16), sh(1, 128, 768), sh(6, 1, 2304), sh(6, 1, 3072), sh(6, 1, 768), sh(1, 24, 768)]
    shapes += [sh(1, b - a) for a, b in zip(CUTS[:-1], CUTS[1:])]
    return pl.pallas_call(
        finish_kernel,
        out_shape=tuple(shapes),
        in_specs=[VMEM] * 7,
        out_specs=(VMEM,) * 14,
        compiler_params=params(),
        name="finish",
    )(*args)


def body(
    inputs, qkv_weight, qkv_bias, out_weight, out_bias, up_weight, up_bias, down_weight, down_bias,
    attn_gain, attn_shift, mlp_gain, mlp_shift, cotangent,
):
    x, g = inputs[0], cotangent[0]
    vectors = (qkv_bias, out_bias, up_bias, down_bias, attn_gain, attn_shift, mlp_gain, mlp_shift)
    ro, rd, zr, dn, o8 = layer(x, g, qkv_weight, up_weight, out_weight, down_weight, *vectors)
    out, dx, qkv, up, ow, dw, *t = finish(x, g, ro, rd, zr, dn, o8)
    qkv, up, ow = qkv.transpose(1, 0, 2), up.transpose(1, 0, 2), ow.transpose(1, 0, 2)
    return out, dx, qkv, t[0], ow, t[1], up, t[2], dw, t[3], t[4], t[5], t[6], t[7]


def solution(mesh):
    tok = P("fsdp", "ctx", None)
    mat = P(None, ("ctx", "fsdp"), None)
    row = P(None, ("ctx", "fsdp"))
    in_specs = (tok, mat, row, mat, row, mat, row, mat, row, row, row, row, row, tok)
    out_specs = (tok, tok, mat, row, mat, row, mat, row, mat, row, row, row, row, row)
    return jax.shard_map(body, mesh=mesh, in_specs=in_specs, out_specs=out_specs, check_vma=False)
```
